32 devices in a mesh: dp: 4 (over z), sp: 8 (over y, x, core).
Axes of the slice: x: 2, y: 2, z: 4, core: 2. Of those that a mesh axis runs over, the one named last changes fastest.
Arguments:
- projected: bfloat16 [4096, 10240], P(('dp', 'sp')), may hold values from -4 to 4
- bias: float32 [10240], replicated, may hold values from -3 to 3
- cotangent: bfloat16 [4096, 8192], P(('dp', 'sp')), may hold values from -4 to 4
- lengths: int32 [4, 4], P('dp'), may hold values from 1 to 512, 1024 in all within a row
- page_source: int32 [4, 64], P('dp'), may hold values from 0 to 63, as said below
Outputs:
- attended: bfloat16 [4096, 8192], P(('dp', 'sp'))
- grad_query: bfloat16 [4096, 8192], P(('dp', 'sp'))
- key_value_gradient: bfloat16 [4096, 2048], P(('dp', 'sp'))
- grad_bias: float32 [10240], replicated
The draws below stay inside these ranges and needn't reach their ends.
Inputs may be any that keep to these rules, and one draw needn't show every extreme that they name: Each row holds the lengths of the 4 sequences of one group in packed order and sums to 1024; the longest is exactly 512. `page_source`: rollout page r of a group lies on the group's device r // 8 at slot r % 8. Each row is a permutation of the group's pages, and no device sends two pages to the same device of its group.
All inputs are finite; a program needn't handle non-finite values.
Results may differ from the reference program's by a relative error of at most 0.012.
Values may be sent and summed in bfloat16 or wider, within the bound.
A program may use at most 192 MiB of HBM per device.

```python
import math
import jax
import jax.numpy as jnp
import numpy as np
from jax import lax

QUERY_HEADS = 64
KEY_VALUE_HEADS = 8
HEAD_DIMENSION = 128
TOK_DEV = 128
SEQS = 4
PAGE = 16
GROUPS = 4
GROUP = 1024
TOKENS = 4096
WIDTH = 10240


def draw_page_source(key, part):
    pages_dev = TOK_DEV // PAGE
    devices = GROUP // TOK_DEV

    def one_group(subkey):
        first_key, second_key, third_key = jax.random.split(subkey, 3)
        device_order = jax.random.permutation(first_key, devices).astype(jnp.int32)
        shifts = jax.random.permutation(second_key, devices)[:pages_dev].astype(jnp.int32)
        slot_order = jax.random.permutation(third_key, pages_dev).astype(jnp.int32)
        target = jnp.arange(devices, dtype=jnp.int32)[:, None]
        source = device_order[(target + shifts[None, :]) % devices]
        place = (slot_order[None, :] + source) % pages_dev
        return (source * pages_dev + place).reshape(devices * pages_dev).astype(jnp.int32)
    return jax.vmap(one_group)(jax.random.split(jax.random.fold_in(key, 17), GROUPS))


def levels(stream_key, dims, shards, least, largest):
    def one(dim, blocks):
        draws = jax.random.uniform(jax.random.fold_in(jax.random.fold_in(stream_key, 6), dim), (blocks,), jnp.float32, least / len(shards), largest / len(shards))
        return jnp.repeat(jnp.exp(draws), dims[dim] // blocks).reshape((-1,) + (1,) * (len(dims) - dim - 1))

    loudness = one(*shards[0])
    for cut in shards[1:]:
        loudness = loudness * one(*cut)
    return loudness


def length_profile(amount, total, limit, skew):
    portions = [(1 << 20) // math.isqrt(grade ** skew) + 1 for grade in range(2, amount + 1)]
    spare, holding = total - limit - (amount - 1), [1] * (amount - 1)
    while spare > 0:
        candidates = [i for i in range(amount - 1) if holding[i] < limit]
        mass, remaining = sum([portions[i] for i in candidates]), spare
        for i in candidates:
            addition = min(limit - holding[i], max(1, remaining * portions[i] // mass), spare)
            holding[i] = holding[i] + addition
            spare = spare - addition
    return np.array([limit] + holding)


def ragged_sizes(own_key, number_of, total, limit, slope):
    if number_of == 2:
        one = jax.random.randint(own_key, (), max(1, total - limit), min(limit, total - 1) + 1)
        return jnp.stack([one, total - one])
    sizes = jnp.asarray(length_profile(number_of, total, limit, slope), jnp.int32)
    couples = (number_of - 1) // 2
    source_of, sink = sizes[1:1 + 2 * couples:2], sizes[2:2 + 2 * couples:2]
    room = jnp.minimum(source_of - 1, limit - sink)
    passed = jax.random.randint(jax.random.fold_in(own_key, 1), (couples,), 0, 1 << 20) % (room + 1)
    sizes = sizes.at[1:1 + 2 * couples:2].set(source_of - passed).at[2:2 + 2 * couples:2].set(sink + passed)
    return sizes[jax.random.permutation(jax.random.fold_in(own_key, 2), number_of)]


def noise(own_key, dims, spread, reach, cuts=(), held_as=jnp.bfloat16):
    entries = jax.random.normal(own_key, dims, jnp.float32) * spread
    if len(cuts) > 0:
        entries = levels(own_key, dims, cuts, -0.22, 0.18) * entries
    return jnp.clip(entries, min=-reach, max=reach).astype(held_as)


def setup_inputs(seed: int = 0) -> dict:
    streams_of = jax.random.split(jax.random.key(seed), 6)
    return {
        "projected": noise(streams_of[0], (TOKENS, WIDTH), 1.0, 4.0, ((0, 32),)),
        "bias": noise(streams_of[1], (WIDTH,), 0.5, 3.0, (), jnp.float32),
        "cotangent": noise(streams_of[2], (TOKENS, QUERY_HEADS * HEAD_DIMENSION), 1.0, 4.0, ((0, 32),)),
        "lengths": jax.vmap(lambda own: ragged_sizes(own, SEQS, GROUP, GROUP // 2, 2))(jax.random.split(streams_of[3], GROUPS)).reshape((GROUPS, SEQS)).astype(jnp.int32),
        "page_source": draw_page_source(jax.random.fold_in(streams_of[5], 71), 0),
    }


rope_base = 1000000.0


def rope_tables(positions, head_size):
    half_size = head_size // 2
    exponent = jnp.arange(half_size, dtype=jnp.float32) * 2.0 / head_size
    frequency = jnp.power(jnp.float32(rope_base), -exponent)
    angles = positions.astype(jnp.float32)[:, None] * frequency[None, :]
    cosine_table = jnp.cos(angles)
    sine_table = jnp.sin(angles)
    return jnp.concatenate([cosine_table, cosine_table], 1), jnp.concatenate([sine_table, sine_table], 1)


def turn_half(tensor_in):
    half_size = tensor_in.shape[-1] // 2
    return jnp.concatenate([-tensor_in[..., half_size:], tensor_in[..., :half_size]], -1)


def apply_rotary(tensor_in, cosine_table, sine_table):
    return tensor_in * cosine_table[:, None, :] + turn_half(tensor_in) * sine_table[:, None, :]


def unrotate(tensor_in, cosine_table, sine_table):
    return tensor_in * cosine_table[:, None, :] - turn_half(tensor_in) * sine_table[:, None, :]


def segments_of(seq_lengths, token_total_count):
    seq_ends = jnp.cumsum(seq_lengths).astype(jnp.int32)
    seq_starts = seq_ends - seq_lengths
    tokens_at = jnp.arange(token_total_count, dtype=jnp.int32)
    segment = jnp.sum((tokens_at[:, None] >= seq_ends[None, :]).astype(jnp.int32), 1)
    labels = jnp.arange(seq_lengths.shape[0], dtype=jnp.int32)
    first_token = jnp.sum(jnp.where(segment[:, None] == labels[None, :], seq_starts[None, :], 0), 1)
    return segment, tokens_at - first_token, first_token


def rounded_duplicate(tensor_in):
    return lax.optimization_barrier(tensor_in.astype(jnp.bfloat16))


def attend_head(inputs, keep):
    query_rows, key_rows, value_rows, upstream_gradient = inputs
    score_scale = HEAD_DIMENSION ** -0.5
    query_wide = query_rows.astype(jnp.float32)
    key_wide = key_rows.astype(jnp.float32)
    value_wide = value_rows.astype(jnp.float32)
    upstream_wide = upstream_gradient.astype(jnp.float32)
    scores = jnp.einsum("qgd,kd->gqk", query_wide, key_wide) * score_scale
    weights = jnp.where(keep[None], jnp.exp(scores), 0.0)
    totals = jnp.sum(weights, 2)
    probs = weights / totals[:, :, None]
    rounded = rounded_duplicate(probs).astype(jnp.float32)
    attended = rounded_duplicate(jnp.einsum("gqk,kd->qgd", rounded, value_wide))
    delta = jnp.transpose(jnp.sum(upstream_wide * attended.astype(jnp.float32), 2))
    dprobs = jnp.einsum("qgd,kd->gqk", upstream_wide, value_wide)
    dscores = rounded_duplicate(probs * (dprobs - delta[:, :, None])).astype(jnp.float32)
    rot_query = jnp.einsum("gqk,kd->qgd", dscores, key_wide) * score_scale
    rot_key = jnp.einsum("gqk,qgd->kd", dscores, query_wide) * score_scale
    grad_value = jnp.einsum("gqk,qgd->kd", rounded, upstream_wide)
    return attended, rot_query, rot_key, grad_value


def one_group(inputs, bias):
    rows_in, upstream_gradient, seq_lengths, page_table = inputs
    token_total_count = rows_in.shape[0]
    row_width = rows_in.shape[1]
    query_span_width = QUERY_HEADS * HEAD_DIMENSION
    key_value_width = KEY_VALUE_HEADS * HEAD_DIMENSION
    heads_per_group = QUERY_HEADS // KEY_VALUE_HEADS
    packed = rows_in.reshape(token_total_count // PAGE, PAGE, row_width)[page_table].reshape(token_total_count, row_width)
    segment, position, first_token = segments_of(seq_lengths, token_total_count)
    cosine_table, sine_table = rope_tables(position, HEAD_DIMENSION)
    query_matrix = packed[:, :query_span_width].astype(jnp.float32) + bias[:query_span_width]
    query_matrix = rounded_duplicate(apply_rotary(query_matrix.reshape(token_total_count, QUERY_HEADS, HEAD_DIMENSION), cosine_table, sine_table))
    every_key = packed[:, query_span_width:query_span_width + key_value_width].astype(jnp.float32) + bias[query_span_width:query_span_width + key_value_width]
    every_key = rounded_duplicate(apply_rotary(every_key.reshape(token_total_count, KEY_VALUE_HEADS, HEAD_DIMENSION), cosine_table, sine_table))
    every_value = rounded_duplicate(packed[:, query_span_width + key_value_width:].astype(jnp.float32) + bias[query_span_width + key_value_width:])
    every_value = every_value.reshape(token_total_count, KEY_VALUE_HEADS, HEAD_DIMENSION)
    tokens_at = jnp.arange(token_total_count, dtype=jnp.int32)
    keep = (segment[:, None] == segment[None, :]) & (tokens_at[:, None] >= tokens_at[None, :])
    head_inputs = (
        jnp.transpose(query_matrix.reshape(token_total_count, KEY_VALUE_HEADS, heads_per_group, HEAD_DIMENSION), (1, 0, 2, 3)),
        jnp.transpose(every_key, (1, 0, 2)),
        jnp.transpose(every_value, (1, 0, 2)),
        jnp.transpose(upstream_gradient.reshape(token_total_count, KEY_VALUE_HEADS, heads_per_group, HEAD_DIMENSION), (1, 0, 2, 3)),
    )
    attended, rot_query, rot_key, grad_value = lax.map(lambda item: attend_head(item, keep), head_inputs)
    attended = jnp.transpose(attended, (1, 0, 2, 3)).reshape(token_total_count, query_span_width)
    rot_query = jnp.transpose(rot_query, (1, 0, 2, 3)).reshape(token_total_count, QUERY_HEADS, HEAD_DIMENSION)
    grad_query = unrotate(rot_query, cosine_table, sine_table).astype(jnp.bfloat16).reshape(token_total_count, query_span_width)
    grad_key = unrotate(jnp.transpose(rot_key, (1, 0, 2)), cosine_table, sine_table).reshape(token_total_count, key_value_width)
    grad_value = jnp.transpose(grad_value, (1, 0, 2)).reshape(token_total_count, key_value_width)
    key_value_gradient = jnp.concatenate([grad_key, grad_value], 1).astype(jnp.bfloat16)
    return attended, grad_query, key_value_gradient


def reference(projected, bias, cotangent, lengths, page_source):
    group_count = lengths.shape[0]
    token_total_count = projected.shape[0] // group_count
    inputs = (
        projected.reshape(group_count, token_total_count, projected.shape[1]),
        cotangent.reshape(group_count, token_total_count, cotangent.shape[1]),
        lengths,
        page_source,
    )
    attended, grad_query, key_value_gradient = lax.map(lambda item: one_group(item, bias), inputs)
    attended = attended.reshape(projected.shape[0], QUERY_HEADS * HEAD_DIMENSION)
    grad_query = grad_query.reshape(projected.shape[0], QUERY_HEADS * HEAD_DIMENSION)
    key_value_gradient = key_value_gradient.reshape(projected.shape[0], 2 * KEY_VALUE_HEADS * HEAD_DIMENSION)
    grad_bias = jnp.concatenate([jnp.sum(grad_query.astype(jnp.float32), 0), jnp.sum(key_value_gradient.astype(jnp.float32), 0)])
    return attended, grad_query, key_value_gradient, grad_bias
```

```python
import functools

import jax
import jax.numpy as jnp
from jax import lax
from jax.experimental import pallas as pl
from jax.experimental.pallas import tpu as pltpu
from jax.sharding import PartitionSpec as P

QUERY_HEADS = 64
KEY_VALUE_HEADS = 8
HEAD_DIMENSION = 128
PAGE = 16
QBLK = 512


rope_base = 1000000.0


def rope_tables(positions, head_size):
    half_size = head_size // 2
    exponent = jnp.arange(half_size, dtype=jnp.float32) * 2.0 / head_size
    frequency = jnp.power(jnp.float32(rope_base), -exponent)
    angles = positions.astype(jnp.float32)[:, None] * frequency[None, :]
    cosine_table = jnp.cos(angles)
    sine_table = jnp.sin(angles)
    return (
        jnp.concatenate([cosine_table, cosine_table], 1),
        jnp.concatenate([sine_table, sine_table], 1),
    )


def turn_half(tensor_in):
    half_size = tensor_in.shape[-1] // 2
    return jnp.concatenate([-tensor_in[..., half_size:], tensor_in[..., :half_size]], -1)


def apply_rotary(tensor_in, cosine_table, sine_table):
    return tensor_in * cosine_table[:, None, :] + turn_half(tensor_in) * sine_table[:, None, :]


def unrotate(tensor_in, cosine_table, sine_table):
    return tensor_in * cosine_table[:, None, :] - turn_half(tensor_in) * sine_table[:, None, :]


def segments_of(seq_lengths, token_total_count):
    seq_ends = jnp.cumsum(seq_lengths)
    seq_starts = seq_ends - seq_lengths
    tokens_at = jnp.arange(token_total_count, dtype=jnp.int32)
    segment = jnp.sum((tokens_at[:, None] >= seq_ends[None, :]).astype(jnp.int32), 1)
    labels = jnp.arange(seq_lengths.shape[0], dtype=jnp.int32)
    first_token = jnp.sum(jnp.where(segment[:, None] == labels[None, :], seq_starts[None, :], 0), 1)
    return (segment, tokens_at - first_token, first_token)


def shards(projected, bias, cotangent, lengths, page_source):
    shard_rows, row_width = projected.shape
    partition_count = lax.axis_size("sp")
    my_index = lax.axis_index("sp")
    group_rows = shard_rows * partition_count
    pages_dev = shard_rows // PAGE
    query_span_width = QUERY_HEADS * HEAD_DIMENSION
    key_value_width = KEY_VALUE_HEADS * HEAD_DIMENSION
    heads_dev = QUERY_HEADS // partition_count
    head_copies = partition_count // KEY_VALUE_HEADS
    page_table = page_source[0]
    page_grid = page_table.reshape(partition_count, pages_dev)
    source_dev = page_grid // pages_dev
    source_slot = page_grid % pages_dev
    from_here = source_dev == my_index
    pick_slot = jnp.sum(jnp.where(from_here, source_slot, 0), 1)
    present = jnp.any(from_here, 1)
    local_pages = projected.reshape(pages_dev, PAGE, row_width)
    outgoing = jnp.where(
        present[:, None, None], local_pages[pick_slot], jnp.zeros((), projected.dtype)
    )
    incoming = lax.all_to_all(outgoing, "sp", split_axis=0, concat_axis=0, tiled=True)
    own_sources = lax.dynamic_slice_in_dim(source_dev, my_index, 1, 0)[0]
    trainer_rows = incoming[own_sources].reshape(shard_rows, row_width)
    query_part = trainer_rows[:, :query_span_width]
    key_part = trainer_rows[:, query_span_width : query_span_width + key_value_width].reshape(
        shard_rows, KEY_VALUE_HEADS, 1, HEAD_DIMENSION
    )
    value_portion = trainer_rows[:, query_span_width + key_value_width :].reshape(
        shard_rows, KEY_VALUE_HEADS, 1, HEAD_DIMENSION
    )
    joined_rows = jnp.concatenate([key_part, value_portion], 3)
    repeated_heads = jnp.broadcast_to(
        joined_rows, (shard_rows, KEY_VALUE_HEADS, head_copies, 2 * HEAD_DIMENSION)
    ).reshape(shard_rows, partition_count * 2 * HEAD_DIMENSION)
    head_query, head_pair, head_upstream = (
        lax.all_to_all(query_part, "sp", split_axis=1, concat_axis=0, tiled=True),
        lax.all_to_all(repeated_heads, "sp", split_axis=1, concat_axis=0, tiled=True),
        lax.all_to_all(cotangent, "sp", split_axis=1, concat_axis=0, tiled=True),
    )
    kv_head = my_index // head_copies
    query_bias = lax.dynamic_slice_in_dim(
        bias, my_index * heads_dev * HEAD_DIMENSION, heads_dev * HEAD_DIMENSION
    )
    key_bias = lax.dynamic_slice_in_dim(
        bias, query_span_width + kv_head * HEAD_DIMENSION, HEAD_DIMENSION
    )
    value_bias = lax.dynamic_slice_in_dim(
        bias, query_span_width + key_value_width + kv_head * HEAD_DIMENSION, HEAD_DIMENSION
    )
    segment, position, first_token = segments_of(lengths[0], group_rows)
    cosine_table, sine_table = rope_tables(position, HEAD_DIMENSION)
    query_matrix = head_query.astype(jnp.float32).reshape(
        group_rows, heads_dev, HEAD_DIMENSION
    ) + query_bias.reshape(heads_dev, HEAD_DIMENSION)
    query_matrix = apply_rotary(query_matrix, cosine_table, sine_table).astype(jnp.bfloat16)
    key_rows = head_pair[:, :HEAD_DIMENSION].astype(jnp.float32) + key_bias
    key_rows = apply_rotary(key_rows[:, None, :], cosine_table, sine_table)[:, 0].astype(
        jnp.bfloat16
    )
    value_rows = (head_pair[:, HEAD_DIMENSION:].astype(jnp.float32) + value_bias).astype(
        jnp.bfloat16
    )
    block_count = group_rows // QBLK
    score_scale = HEAD_DIMENSION ** (-0.5)
    query_blocks = query_matrix.reshape(block_count, QBLK, heads_dev, HEAD_DIMENSION)
    key_blocks = key_rows.reshape(block_count, QBLK, HEAD_DIMENSION)
    value_blocks = value_rows.reshape(block_count, QBLK, HEAD_DIMENSION)
    segment_blocks = segment.reshape(block_count, QBLK)
    token_blocks = jnp.arange(group_rows, dtype=jnp.int32).reshape(block_count, QBLK)
    upstream_gradient = head_upstream.reshape(block_count, QBLK, heads_dev, HEAD_DIMENSION)

    def weights(row_block, col_block):
        scores = (
            jnp.einsum(
                "qhd,kd->hqk",
                query_blocks[row_block],
                key_blocks[col_block],
                preferred_element_type=jnp.float32,
            )
            * score_scale
        )
        keep = (segment_blocks[row_block][:, None] == segment_blocks[col_block][None, :]) & (
            token_blocks[row_block][:, None] >= token_blocks[col_block][None, :]
        )
        return jnp.where(keep[None], jnp.exp(scores), 0.0)

    zero_rows = jnp.zeros((heads_dev, QBLK), jnp.float32)
    totals = []
    for row_block in range(block_count):
        running = zero_rows
        for col_block in range(row_block + 1):
            running = running + jnp.sum(weights(row_block, col_block), 2)
        totals.append(running)
    zero_out = jnp.zeros((QBLK, heads_dev, HEAD_DIMENSION), jnp.float32)
    attended_blocks = []
    for row_block in range(block_count):
        running = zero_out
        for col_block in range(row_block + 1):
            attend_probs = (weights(row_block, col_block) / totals[row_block][:, :, None]).astype(
                jnp.bfloat16
            )
            running = running + jnp.einsum(
                "hqk,kd->qhd",
                attend_probs,
                value_blocks[col_block],
                preferred_element_type=jnp.float32,
            )
        attended_blocks.append(running.astype(jnp.bfloat16))
    attended = jnp.stack(attended_blocks)
    attended_out = lax.all_to_all(
        attended.reshape(group_rows, heads_dev * HEAD_DIMENSION),
        "sp",
        split_axis=0,
        concat_axis=1,
        tiled=True,
    )
    zero_key = jnp.zeros((QBLK, HEAD_DIMENSION), jnp.float32)
    key_grads = [zero_key for col_block in range(block_count)]
    value_grads = [zero_key for col_block in range(block_count)]
    query_grads = []
    for row_block in range(block_count):
        delta = jnp.transpose(
            jnp.sum(
                upstream_gradient[row_block].astype(jnp.float32)
                * attended[row_block].astype(jnp.float32),
                2,
            )
        )
        running = zero_out
        for col_block in range(row_block + 1):
            probs = weights(row_block, col_block) / totals[row_block][:, :, None]
            rounded = probs.astype(jnp.bfloat16)
            dprobs = jnp.einsum(
                "qhd,kd->hqk",
                upstream_gradient[row_block],
                value_blocks[col_block],
                preferred_element_type=jnp.float32,
            )
            dscores = (probs * (dprobs - delta[:, :, None])).astype(jnp.bfloat16)
            part_query = (
                jnp.einsum(
                    "hqk,kd->qhd",
                    dscores,
                    key_blocks[col_block],
                    preferred_element_type=jnp.float32,
                )
                * score_scale
            )
            part_key = (
                jnp.einsum(
                    "hqk,qhd->kd",
                    dscores,
                    query_blocks[row_block],
                    preferred_element_type=jnp.float32,
                )
                * score_scale
            )
            part_value = jnp.einsum(
                "hqk,qhd->kd",
                rounded,
                upstream_gradient[row_block],
                preferred_element_type=jnp.float32,
            )
            part_query, part_key, part_value = (part_query, part_key, part_value)
            running = running + part_query
            key_grads[col_block] = key_grads[col_block] + part_key
            value_grads[col_block] = value_grads[col_block] + part_value
        query_grads.append(running)
    rot_query = jnp.stack(query_grads).reshape(group_rows, heads_dev, HEAD_DIMENSION)
    grad_query = (
        unrotate(rot_query, cosine_table, sine_table)
        .astype(jnp.bfloat16)
        .reshape(group_rows, heads_dev * HEAD_DIMENSION)
    )
    query_out = lax.all_to_all(grad_query, "sp", split_axis=0, concat_axis=1, tiled=True)
    grad_key = unrotate(
        jnp.stack(key_grads).reshape(group_rows, 1, HEAD_DIMENSION), cosine_table, sine_table
    ).reshape(group_rows, HEAD_DIMENSION)
    grad_value = jnp.stack(value_grads).reshape(group_rows, HEAD_DIMENSION)
    pair_grads = jnp.concatenate([grad_key, grad_value], 1)
    pair_gradient_back = lax.all_to_all(pair_grads, "sp", split_axis=0, concat_axis=1, tiled=True)
    pair_gradient_sum = jnp.sum(
        pair_gradient_back.reshape(shard_rows, KEY_VALUE_HEADS, head_copies, 2, HEAD_DIMENSION), 2
    )
    key_value_gradient = (
        jnp.transpose(pair_gradient_sum, (0, 2, 1, 3))
        .reshape(shard_rows, 2 * key_value_width)
        .astype(jnp.bfloat16)
    )
    local_sums = jnp.concatenate(
        [
            jnp.sum(query_out.astype(jnp.float32), 0),
            jnp.sum(key_value_gradient.astype(jnp.float32), 0),
        ]
    )
    grad_bias = lax.psum(local_sums, ("dp", "sp"))
    return (attended_out, query_out, key_value_gradient, grad_bias)


MESH = pl.DeviceIdType.MESH
D = HEAD_DIMENSION
NT = (((1,), (1,)), ((), ()))
NN = (((1,), (0,)), ((), ()))


def dot(left, right, dims=NN):
    return lax.dot_general(left, right, dims, preferred_element_type=jnp.float32)


def fused_kernel(
    n, ndp, heads, rows,
    len_ref, page_ref, proj_ref, cot_ref, bias_ref, freq_ref,
    att_out, gq_out, kvg_out, gb_out,
    recv_q, recv_c, recv_kv, perm, key_rows, value_rows, key_t, value_t,
    cos_t, sin_t, mask_t, att_buf, gq_buf, kv_buf, dk, dv, sums, dp_buf, total, gb_all,
    in_send, in_recv, kv_send, kv_recv, out_send, out_recv, kvo_send, kvo_recv,
    dp_send, dp_recv, gb_send, gb_recv,
):
    me = lax.axis_index("sp")
    mine = lax.axis_index("dp")
    group = n * rows
    pages = group // PAGE
    block = 256
    window = group // 2
    scale = D ** (-0.5)
    key_base = QUERY_HEADS * D
    value_base = key_base + KEY_VALUE_HEADS * D
    my_rows = pl.ds(pl.multiple_of(me * rows, rows), rows)

    def columns(start):
        return pl.ds(pl.multiple_of(start, D), D)

    def sp_peer(o):
        return lax.rem(me + o, n)

    def dp_peer(o):
        return lax.rem(mine + o, ndp)

    def peer_rows(o):
        return pl.ds(pl.multiple_of(sp_peer(o) * rows, rows), rows)

    def move(src, dst, send, recv, o):
        if o == 0:
            return pltpu.make_async_copy(src, dst, recv)
        return pltpu.make_async_remote_copy(
            src_ref=src, dst_ref=dst, send_sem=send, recv_sem=recv,
            device_id={"sp": sp_peer(o)}, device_id_type=MESH,
        )

    def head_in(kind, h, o):
        ref, land = ((proj_ref, recv_q), (cot_ref, recv_c))[kind]
        return move(
            ref.at[:, columns((sp_peer(o) * heads + h) * D)],
            land.at[h, my_rows, :],
            in_send.at[kind, h, o], in_recv.at[kind, h, o], o,
        )

    def pair_in(kind, o):
        base = (key_base, value_base)[kind]
        return move(
            proj_ref.at[:, columns(base + sp_peer(o) * D)],
            recv_kv.at[kind, my_rows, :],
            kv_send.at[kind, o], kv_recv.at[kind, o], o,
        )

    def head_out(kind, h, o):
        ref, land = ((att_buf, att_out), (gq_buf, gq_out))[kind]
        return move(
            ref.at[h, peer_rows(o), :],
            land.at[:, columns((me * heads + h) * D)],
            out_send.at[kind, h, o], out_recv.at[kind, h, o], o,
        )

    def pair_out(kind, o):
        return move(
            kv_buf.at[kind, peer_rows(o), :],
            kvg_out.at[:, columns(kind * KEY_VALUE_HEADS * D + me * D)],
            kvo_send.at[kind, o], kvo_recv.at[kind, o], o,
        )

    def sums_dp(o):
        return pltpu.make_async_remote_copy(
            src_ref=sums, dst_ref=dp_buf.at[mine],
            send_sem=dp_send.at[o], recv_sem=dp_recv.at[o],
            device_id={"dp": dp_peer(o)}, device_id_type=MESH,
        )

    def sums_sp(o):
        return pltpu.make_async_remote_copy(
            src_ref=total, dst_ref=gb_all.at[me],
            send_sem=gb_send.at[o], recv_sem=gb_recv.at[o],
            device_id={"sp": sp_peer(o)}, device_id_type=MESH,
        )

    def arrive(copy, o):
        if o == 0:
            copy.wait()
        else:
            copy.wait_recv()

    barrier = pltpu.get_barrier_semaphore()
    for o in range(1, n):
        pl.semaphore_signal(barrier, inc=1, device_id={"sp": sp_peer(o)}, device_id_type=MESH)
    for o in range(1, ndp):
        pl.semaphore_signal(barrier, inc=1, device_id={"dp": dp_peer(o)}, device_id_type=MESH)
    pl.semaphore_wait(barrier, n - 1 + ndp - 1)

    for kind in range(2):
        for o in range(n):
            pair_in(kind, o).start()

    def send_head(h, carry):
        for kind in range(2):
            for o in range(n):
                head_in(kind, h, o).start()
        return carry

    lax.fori_loop(0, heads, send_head, 0)

    starts = []
    begin = jnp.int32(0)
    for s in range(len_ref.shape[1] - 1):
        begin = begin + len_ref[0, s]
        starts.append(begin)

    def first_of(token):
        first = jnp.zeros_like(token)
        for start in starts:
            first = jnp.where(token >= start, start, first)
        return first

    def table_block(i, carry):
        at = pl.ds(pl.multiple_of(i * 128, 128), 128)
        token = lax.broadcasted_iota(jnp.int32, (128, D), 0) + i * 128
        lane = lax.broadcasted_iota(jnp.int32, (128, D), 1)
        angle = (token - first_of(token)).astype(jnp.float32) * freq_ref[...]
        cos_t[at, :] = jnp.cos(angle)
        sine = jnp.sin(angle)
        sin_t[at, :] = jnp.where(lane < D // 2, -sine, sine)
        return carry

    lax.fori_loop(0, group // 128, table_block, 0)

    spans = []
    offset = 0
    for i in range(group // block):
        low = max(0, (i * block - window + 1) // block * block)
        spans.append((i * block, low, (i + 1) * block, offset))
        offset += (i + 1) * block - low
    for top, low, high, offset in spans:
        query_at = lax.broadcasted_iota(jnp.int32, (1, block), 1) + top
        first = first_of(query_at)
        key_at = lax.broadcasted_iota(jnp.int32, (high - low, block), 0) + low
        keep = (key_at >= first) & (key_at <= query_at)
        mask_t[offset : offset + high - low, :] = jnp.where(keep, 0.0, -jnp.inf)

    for page in range(pages):
        source = page_ref[0, page] * PAGE
        sub = lax.broadcasted_iota(jnp.int32, (PAGE, group), 0)
        lane = lax.broadcasted_iota(jnp.int32, (PAGE, group), 1)
        perm[page * PAGE : (page + 1) * PAGE, :] = jnp.where(lane - sub == source, 1.0, 0.0).astype(
            jnp.bfloat16
        )

    def rope(x, at):
        return x * cos_t[at, :] + pltpu.roll(x, D // 2, 1) * sin_t[at, :]

    def unrope(x, at):
        return x * cos_t[at, :] - pltpu.roll(x, D // 2, 1) * sin_t[at, :]

    for kind in range(2):
        for o in range(n):
            arrive(pair_in(kind, o), o)
    key_bias = bias_ref[pl.ds(QUERY_HEADS + me, 1), :]
    value_bias = bias_ref[pl.ds(QUERY_HEADS + KEY_VALUE_HEADS + me, 1), :]
    for top, _, high, _ in spans:
        at = slice(top, high)
        rotated = rope(dot(perm[at, :], recv_kv[0]) + key_bias, at)
        key_rows[at, :] = rotated.astype(jnp.bfloat16)
        key_t[:, at] = rotated.T.astype(jnp.bfloat16)
    for top, _, high, _ in spans:
        at = slice(top, high)
        shifted = dot(perm[at, :], recv_kv[1]) + value_bias
        value_rows[at, :] = shifted.astype(jnp.bfloat16)
        value_t[:, at] = shifted.T.astype(jnp.bfloat16)
    dk[...] = jnp.zeros_like(dk)
    dv[...] = jnp.zeros_like(dv)
    sums[...] = jnp.zeros_like(sums)

    def one_head(h, carry):
        for kind in range(2):
            for o in range(n):
                arrive(head_in(kind, h, o), o)
        query_bias = bias_ref[pl.ds(me * heads + h, 1), :]
        column_sum = jnp.zeros((1, D), jnp.float32)
        for top, low, high, offset in spans:
            at, keys = slice(top, high), slice(low, high)
            query = rope(dot(perm[at, :], recv_q[h]) + query_bias, at).astype(jnp.bfloat16)
            upstream = recv_c[h, at, :]
            upstream_t = upstream.astype(jnp.float32).T
            scores = dot(key_rows[keys, :], query, NT) * scale
            weights = jnp.exp(scores + mask_t[offset : offset + high - low, :])
            totals = jnp.sum(weights, 0, keepdims=True)
            shrink = jnp.where(totals > 1e37, 0.015625, 1.0)
            probs = (weights * shrink) * (1.0 / (totals * shrink))
            rounded = probs.astype(jnp.bfloat16)
            attended_t = dot(value_t[:, keys], rounded)
            att_buf[h, at, :] = attended_t.T.astype(jnp.bfloat16)
            kept = attended_t.astype(jnp.bfloat16).astype(jnp.float32)
            delta = jnp.sum(upstream_t * kept, 0, keepdims=True)
            dprobs = dot(value_rows[keys, :], upstream, NT)
            dscores = (probs * (dprobs - delta)).astype(jnp.bfloat16)
            rot_query = dot(key_t[:, keys], dscores).T * scale
            grad_query = unrope(rot_query, at).astype(jnp.bfloat16)
            gq_buf[h, at, :] = grad_query
            column_sum += jnp.sum(grad_query.astype(jnp.float32), 0, keepdims=True)
            dk[keys, :] += dot(dscores, query)
            dv[keys, :] += dot(rounded, upstream)
        sums[pl.ds(h, 1), :] = column_sum
        for kind in range(2):
            for o in range(n):
                head_out(kind, h, o).start()
        return carry

    lax.fori_loop(0, heads, one_head, 0)

    key_sum = jnp.zeros((1, D), jnp.float32)
    value_sum = jnp.zeros((1, D), jnp.float32)
    for top, _, high, _ in spans:
        at = slice(top, high)
        grad_key = unrope(dk[at, :] * scale, at).astype(jnp.bfloat16)
        grad_value = dv[at, :].astype(jnp.bfloat16)
        kv_buf[0, at, :] = grad_key
        kv_buf[1, at, :] = grad_value
        key_sum += jnp.sum(grad_key.astype(jnp.float32), 0, keepdims=True)
        value_sum += jnp.sum(grad_value.astype(jnp.float32), 0, keepdims=True)
    sums[heads : heads + 1, :] = key_sum
    sums[heads + 1 : heads + 2, :] = value_sum
    for o in range(1, ndp):
        sums_dp(o).start()
    for kind in range(2):
        for o in range(n):
            pair_out(kind, o).start()
    dp_buf[mine] = sums[...]
    for o in range(1, ndp):
        sums_dp(o).wait()
    running = dp_buf[0]
    for d in range(1, ndp):
        running = running + dp_buf[d]
    total[...] = running
    for o in range(1, n):
        sums_sp(o).start()
    gb_all[me] = running
    for o in range(1, n):
        sums_sp(o).wait()
    gb_out[...] = gb_all[...]

    for kind in range(2):
        for o in range(n):
            pair_out(kind, o).wait()
            if o > 0:
                pair_in(kind, o).wait_send()

    def drain(h, carry):
        for kind in range(2):
            for o in range(n):
                head_out(kind, h, o).wait()
                if o > 0:
                    head_in(kind, h, o).wait_send()
        return carry

    lax.fori_loop(0, heads, drain, 0)


def fused_shards(projected, bias, cotangent, lengths, page_source):
    rows, _ = projected.shape
    n = lax.axis_size("sp")
    ndp = lax.axis_size("dp")
    heads = QUERY_HEADS // n
    group = n * rows
    block, window = 256, group // 2
    mask_rows = sum(
        (i + 1) * block - max(0, (i * block - window + 1) // block * block)
        for i in range(group // block)
    )
    exponent = jnp.arange(D // 2, dtype=jnp.float32) * 2.0 / D
    frequency = jnp.power(jnp.float32(rope_base), -exponent)
    frequency = jnp.concatenate([frequency, frequency])[None, :]
    sum_rows = heads + 8
    f32, bf16 = jnp.float32, jnp.bfloat16
    dma = pltpu.SemaphoreType.DMA
    anywhere = pl.BlockSpec(memory_space=pl.ANY)
    scalars = pl.BlockSpec(memory_space=pltpu.SMEM)
    vector = pl.BlockSpec(memory_space=pltpu.VMEM)
    attended, grad_query, pair_gradient, bias_sums = pl.pallas_call(
        functools.partial(fused_kernel, n, ndp, heads, rows),
        out_shape=(
            jax.ShapeDtypeStruct((rows, QUERY_HEADS * D), bf16),
            jax.ShapeDtypeStruct((rows, QUERY_HEADS * D), bf16),
            jax.ShapeDtypeStruct((rows, 2 * KEY_VALUE_HEADS * D), bf16),
            jax.ShapeDtypeStruct((n, sum_rows, D), f32),
        ),
        in_specs=[scalars, scalars, anywhere, anywhere, vector, vector],
        out_specs=(anywhere, anywhere, anywhere, vector),
        scratch_shapes=[
            pltpu.VMEM((heads, group, D), bf16),
            pltpu.VMEM((heads, group, D), bf16),
            pltpu.VMEM((2, group, D), bf16),
            pltpu.VMEM((group, group), bf16),
            pltpu.VMEM((group, D), bf16),
            pltpu.VMEM((group, D), bf16),
            pltpu.VMEM((D, group), bf16),
            pltpu.VMEM((D, group), bf16),
            pltpu.VMEM((group, D), f32),
            pltpu.VMEM((group, D), f32),
            pltpu.VMEM((mask_rows, block), f32),
            pltpu.VMEM((heads, group, D), bf16),
            pltpu.VMEM((heads, group, D), bf16),
            pltpu.VMEM((2, group, D), bf16),
            pltpu.VMEM((group, D), f32),
            pltpu.VMEM((group, D), f32),
            pltpu.VMEM((sum_rows, D), f32),
            pltpu.VMEM((ndp, sum_rows, D), f32),
            pltpu.VMEM((sum_rows, D), f32),
            pltpu.VMEM((n, sum_rows, D), f32),
            dma((2, heads, n)), dma((2, heads, n)), dma((2, n)), dma((2, n)),
            dma((2, heads, n)), dma((2, heads, n)), dma((2, n)), dma((2, n)),
            dma((ndp,)), dma((ndp,)), dma((n,)), dma((n,)),
        ],
        compiler_params=pltpu.CompilerParams(
            collective_id=0, has_side_effects=True, vmem_limit_bytes=56 * 1024 * 1024
        ),
        cost_estimate=pl.CostEstimate(
            flops=14 * heads * group * window * D,
            bytes_accessed=4 * rows * 36864,
            transcendentals=heads * group * window,
        ),
    )(lengths, page_source, projected, cotangent, bias.reshape(-1, D), frequency)
    grad_bias = jnp.concatenate(
        [
            bias_sums[:, :heads].reshape(-1),
            bias_sums[:, heads].reshape(-1),
            bias_sums[:, heads + 1].reshape(-1),
        ]
    )
    return attended, grad_query, pair_gradient, grad_bias


def solution(mesh):
    in_specs = (P(("dp", "sp"), None), P(), P(("dp", "sp"), None), P("dp", None), P("dp", None))
    out_specs = (P(("dp", "sp"), None), P(("dp", "sp"), None), P(("dp", "sp"), None), P())
    body = fused_shards if mesh.shape["sp"] == KEY_VALUE_HEADS else shards
    return jax.shard_map(body, mesh=mesh, in_specs=in_specs, out_specs=out_specs, check_vma=False)
```

```python
import functools

import jax
import jax.numpy as jnp
from jax import lax
from jax.experimental import pallas as pl
from jax.experimental.pallas import tpu as pltpu
from jax.sharding import PartitionSpec as P

QUERY_HEADS = 64
KEY_VALUE_HEADS = 8
HEAD_DIMENSION = 128
PAGE = 16
QBLK = 512


rope_base = 1000000.0


def rope_tables(positions, head_size):
    half_size = head_size // 2
    exponent = jnp.arange(half_size, dtype=jnp.float32) * 2.0 / head_size
    frequency = jnp.power(jnp.float32(rope_base), -exponent)
    angles = positions.astype(jnp.float32)[:, None] * frequency[None, :]
    cosine_table = jnp.cos(angles)
    sine_table = jnp.sin(angles)
    return (
        jnp.concatenate([cosine_table, cosine_table], 1),
        jnp.concatenate([sine_table, sine_table], 1),
    )


def turn_half(tensor_in):
    half_size = tensor_in.shape[-1] // 2
    return jnp.concatenate([-tensor_in[..., half_size:], tensor_in[..., :half_size]], -1)


def apply_rotary(tensor_in, cosine_table, sine_table):
    return tensor_in * cosine_table[:, None, :] + turn_half(tensor_in) * sine_table[:, None, :]


def unrotate(tensor_in, cosine_table, sine_table):
    return tensor_in * cosine_table[:, None, :] - turn_half(tensor_in) * sine_table[:, None, :]


def segments_of(seq_lengths, token_total_count):
    seq_ends = jnp.cumsum(seq_lengths)
    seq_starts = seq_ends - seq_lengths
    tokens_at = jnp.arange(token_total_count, dtype=jnp.int32)
    segment = jnp.sum((tokens_at[:, None] >= seq_ends[None, :]).astype(jnp.int32), 1)
    labels = jnp.arange(seq_lengths.shape[0], dtype=jnp.int32)
    first_token = jnp.sum(jnp.where(segment[:, None] == labels[None, :], seq_starts[None, :], 0), 1)
    return (segment, tokens_at - first_token, first_token)


def shards(projected, bias, cotangent, lengths, page_source):
    shard_rows, row_width = projected.shape
    partition_count = lax.axis_size("sp")
    my_index = lax.axis_index("sp")
    group_rows = shard_rows * partition_count
    pages_dev = shard_rows // PAGE
    query_span_width = QUERY_HEADS * HEAD_DIMENSION
    key_value_width = KEY_VALUE_HEADS * HEAD_DIMENSION
    heads_dev = QUERY_HEADS // partition_count
    head_copies = partition_count // KEY_VALUE_HEADS
    page_table = page_source[0]
    page_grid = page_table.reshape(partition_count, pages_dev)
    source_dev = page_grid // pages_dev
    source_slot = page_grid % pages_dev
    from_here = source_dev == my_index
    pick_slot = jnp.sum(jnp.where(from_here, source_slot, 0), 1)
    present = jnp.any(from_here, 1)
    local_pages = projected.reshape(pages_dev, PAGE, row_width)
    outgoing = jnp.where(
        present[:, None, None], local_pages[pick_slot], jnp.zeros((), projected.dtype)
    )
    incoming = lax.all_to_all(outgoing, "sp", split_axis=0, concat_axis=0, tiled=True)
    own_sources = lax.dynamic_slice_in_dim(source_dev, my_index, 1, 0)[0]
    trainer_rows = incoming[own_sources].reshape(shard_rows, row_width)
    query_part = trainer_rows[:, :query_span_width]
    key_part = trainer_rows[:, query_span_width : query_span_width + key_value_width].reshape(
        shard_rows, KEY_VALUE_HEADS, 1, HEAD_DIMENSION
    )
    value_portion = trainer_rows[:, query_span_width + key_value_width :].reshape(
        shard_rows, KEY_VALUE_HEADS, 1, HEAD_DIMENSION
    )
    joined_rows = jnp.concatenate([key_part, value_portion], 3)
    repeated_heads = jnp.broadcast_to(
        joined_rows, (shard_rows, KEY_VALUE_HEADS, head_copies, 2 * HEAD_DIMENSION)
    ).reshape(shard_rows, partition_count * 2 * HEAD_DIMENSION)
    head_query, head_pair, head_upstream = (
        lax.all_to_all(query_part, "sp", split_axis=1, concat_axis=0, tiled=True),
        lax.all_to_all(repeated_heads, "sp", split_axis=1, concat_axis=0, tiled=True),
        lax.all_to_all(cotangent, "sp", split_axis=1, concat_axis=0, tiled=True),
    )
    kv_head = my_index // head_copies
    query_bias = lax.dynamic_slice_in_dim(
        bias, my_index * heads_dev * HEAD_DIMENSION, heads_dev * HEAD_DIMENSION
    )
    key_bias = lax.dynamic_slice_in_dim(
        bias, query_span_width + kv_head * HEAD_DIMENSION, HEAD_DIMENSION
    )
    value_bias = lax.dynamic_slice_in_dim(
        bias, query_span_width + key_value_width + kv_head * HEAD_DIMENSION, HEAD_DIMENSION
    )
    segment, position, first_token = segments_of(lengths[0], group_rows)
    cosine_table, sine_table = rope_tables(position, HEAD_DIMENSION)
    query_matrix = head_query.astype(jnp.float32).reshape(
        group_rows, heads_dev, HEAD_DIMENSION
    ) + query_bias.reshape(heads_dev, HEAD_DIMENSION)
    query_matrix = apply_rotary(query_matrix, cosine_table, sine_table).astype(jnp.bfloat16)
    key_rows = head_pair[:, :HEAD_DIMENSION].astype(jnp.float32) + key_bias
    key_rows = apply_rotary(key_rows[:, None, :], cosine_table, sine_table)[:, 0].astype(
        jnp.bfloat16
    )
    value_rows = (head_pair[:, HEAD_DIMENSION:].astype(jnp.float32) + value_bias).astype(
        jnp.bfloat16
    )
    block_count = group_rows // QBLK
    score_scale = HEAD_DIMENSION ** (-0.5)
    query_blocks = query_matrix.reshape(block_count, QBLK, heads_dev, HEAD_DIMENSION)
    key_blocks = key_rows.reshape(block_count, QBLK, HEAD_DIMENSION)
    value_blocks = value_rows.reshape(block_count, QBLK, HEAD_DIMENSION)
    segment_blocks = segment.reshape(block_count, QBLK)
    token_blocks = jnp.arange(group_rows, dtype=jnp.int32).reshape(block_count, QBLK)
    upstream_gradient = head_upstream.reshape(block_count, QBLK, heads_dev, HEAD_DIMENSION)

    def weights(row_block, col_block):
        scores = (
            jnp.einsum(
                "qhd,kd->hqk",
                query_blocks[row_block],
                key_blocks[col_block],
                preferred_element_type=jnp.float32,
            )
            * score_scale
        )
        keep = (segment_blocks[row_block][:, None] == segment_blocks[col_block][None, :]) & (
            token_blocks[row_block][:, None] >= token_blocks[col_block][None, :]
        )
        return jnp.where(keep[None], jnp.exp(scores), 0.0)

    zero_rows = jnp.zeros((heads_dev, QBLK), jnp.float32)
    totals = []
    for row_block in range(block_count):
        running = zero_rows
        for col_block in range(row_block + 1):
            running = running + jnp.sum(weights(row_block, col_block), 2)
        totals.append(running)
    zero_out = jnp.zeros((QBLK, heads_dev, HEAD_DIMENSION), jnp.float32)
    attended_blocks = []
    for row_block in range(block_count):
        running = zero_out
        for col_block in range(row_block + 1):
            attend_probs = (weights(row_block, col_block) / totals[row_block][:, :, None]).astype(
                jnp.bfloat16
            )
            running = running + jnp.einsum(
                "hqk,kd->qhd",
                attend_probs,
                value_blocks[col_block],
                preferred_element_type=jnp.float32,
            )
        attended_blocks.append(running.astype(jnp.bfloat16))
    attended = jnp.stack(attended_blocks)
    attended_out = lax.all_to_all(
        attended.reshape(group_rows, heads_dev * HEAD_DIMENSION),
        "sp",
        split_axis=0,
        concat_axis=1,
        tiled=True,
    )
    zero_key = jnp.zeros((QBLK, HEAD_DIMENSION), jnp.float32)
    key_grads = [zero_key for col_block in range(block_count)]
    value_grads = [zero_key for col_block in range(block_count)]
    query_grads = []
    for row_block in range(block_count):
        delta = jnp.transpose(
            jnp.sum(
                upstream_gradient[row_block].astype(jnp.float32)
                * attended[row_block].astype(jnp.float32),
                2,
            )
        )
        running = zero_out
        for col_block in range(row_block + 1):
            probs = weights(row_block, col_block) / totals[row_block][:, :, None]
            rounded = probs.astype(jnp.bfloat16)
            dprobs = jnp.einsum(
                "qhd,kd->hqk",
                upstream_gradient[row_block],
                value_blocks[col_block],
                preferred_element_type=jnp.float32,
            )
            dscores = (probs * (dprobs - delta[:, :, None])).astype(jnp.bfloat16)
            part_query = (
                jnp.einsum(
                    "hqk,kd->qhd",
                    dscores,
                    key_blocks[col_block],
                    preferred_element_type=jnp.float32,
                )
                * score_scale
            )
            part_key = (
                jnp.einsum(
                    "hqk,qhd->kd",
                    dscores,
                    query_blocks[row_block],
                    preferred_element_type=jnp.float32,
                )
                * score_scale
            )
            part_value = jnp.einsum(
                "hqk,qhd->kd",
                rounded,
                upstream_gradient[row_block],
                preferred_element_type=jnp.float32,
            )
            part_query, part_key, part_value = (part_query, part_key, part_value)
            running = running + part_query
            key_grads[col_block] = key_grads[col_block] + part_key
            value_grads[col_block] = value_grads[col_block] + part_value
        query_grads.append(running)
    rot_query = jnp.stack(query_grads).reshape(group_rows, heads_dev, HEAD_DIMENSION)
    grad_query = (
        unrotate(rot_query, cosine_table, sine_table)
        .astype(jnp.bfloat16)
        .reshape(group_rows, heads_dev * HEAD_DIMENSION)
    )
    query_out = lax.all_to_all(grad_query, "sp", split_axis=0, concat_axis=1, tiled=True)
    grad_key = unrotate(
        jnp.stack(key_grads).reshape(group_rows, 1, HEAD_DIMENSION), cosine_table, sine_table
    ).reshape(group_rows, HEAD_DIMENSION)
    grad_value = jnp.stack(value_grads).reshape(group_rows, HEAD_DIMENSION)
    pair_grads = jnp.concatenate([grad_key, grad_value], 1)
    pair_gradient_back = lax.all_to_all(pair_grads, "sp", split_axis=0, concat_axis=1, tiled=True)
    pair_gradient_sum = jnp.sum(
        pair_gradient_back.reshape(shard_rows, KEY_VALUE_HEADS, head_copies, 2, HEAD_DIMENSION), 2
    )
    key_value_gradient = (
        jnp.transpose(pair_gradient_sum, (0, 2, 1, 3))
        .reshape(shard_rows, 2 * key_value_width)
        .astype(jnp.bfloat16)
    )
    local_sums = jnp.concatenate(
        [
            jnp.sum(query_out.astype(jnp.float32), 0),
            jnp.sum(key_value_gradient.astype(jnp.float32), 0),
        ]
    )
    grad_bias = lax.psum(local_sums, ("dp", "sp"))
    return (attended_out, query_out, key_value_gradient, grad_bias)


MESH = pl.DeviceIdType.MESH
D = HEAD_DIMENSION
NT = (((1,), (1,)), ((), ()))
NN = (((1,), (0,)), ((), ()))


def dot(left, right, dims=NN):
    return lax.dot_general(left, right, dims, preferred_element_type=jnp.float32)


def fused_kernel(
    n, ndp, rows,
    len_ref, page_ref, proj_ref, cot_ref, bias_ref, freq_ref,
    att_out, gq_out, kvg_out, gb_out,
    out_q, out_kv, recv_q, recv_kv, recv_c, perm_out, perm_q, perm_kv,
    key_rows, value_rows, key_t, value_t, cos_t, sin_t, mask_t, att_buf, gq_buf,
    dk, dv, own_kv, part_kv, got_kv, fin_kv, sums, dp_buf, total, gb_all,
    kv_send, kv_recv, q_send, q_recv, c_send, c_recv, c_here,
    o_send, o_recv, o_here, p_send, p_recv, f_send, f_recv, f_here,
    dp_send, dp_recv, gb_send, gb_recv,
):
    me = lax.axis_index("sp")
    mine = lax.axis_index("dp")
    chip, core = me // 2, lax.rem(me, 2)
    chips = n // 2
    tokens = 2 * rows
    group = n * rows
    share = 2 * PAGE
    pages_dev = rows // PAGE
    back = (group // 2 - 1 + tokens - 1) // tokens
    span = (back + 1) * tokens
    home = back * tokens
    half = QUERY_HEADS // 2
    pairs = KEY_VALUE_HEADS // 2
    copies = half // pairs
    wide = copies * D
    scale = D ** (-0.5)
    key_base = QUERY_HEADS * D
    value_base = key_base + KEY_VALUE_HEADS * D
    query_at = slice(home, span)

    def aligned(start, size):
        return pl.ds(pl.multiple_of(start, size), size)

    def columns(start, size):
        return pl.ds(pl.multiple_of(start, D), size)

    def sp_peer(o):
        return lax.rem(me + o, n)

    def dp_peer(o):
        return lax.rem(mine + o, ndp)

    def move(src, dst, send, recv, target):
        return pltpu.make_async_remote_copy(
            src_ref=src, dst_ref=dst, send_sem=send, recv_sem=recv,
            device_id={"sp": target}, device_id_type=MESH,
        )

    def pair_in(kind, j, o):
        peer = sp_peer(o)
        src = out_kv.at[
            kind * KEY_VALUE_HEADS + lax.rem(peer, 2) * pairs + j,
            pl.ds(pl.multiple_of(peer // 2 * share, share), (back + 1) * share), :,
        ]
        dst = recv_kv.at[kind, j, aligned(me * (back + 1) * share, (back + 1) * share), :]
        if o == 0:
            return pltpu.make_async_copy(src, dst, kv_recv.at[kind, j, 0])
        return move(src, dst, kv_send.at[kind, j, o], kv_recv.at[kind, j, o], peer)

    def query_in(j, o):
        peer = sp_peer(o)
        src = out_q.at[
            pl.ds(lax.rem(peer, 2) * half + j * copies, copies), aligned(peer // 2 * share, share), :
        ]
        dst = recv_q.at[pl.ds(j * copies, copies), aligned(me * share, share), :]
        if o == 0:
            return pltpu.make_async_copy(src, dst, q_recv.at[j, 0])
        return move(src, dst, q_send.at[j, o], q_recv.at[j, o], peer)

    def upstream_in(j, here):
        who = core if here else 1 - core
        src = cot_ref.at[:, columns((who * half + j * copies) * D, wide)]
        dst = recv_c.at[aligned(core * rows, rows), columns(j * wide, wide)]
        if here:
            return pltpu.make_async_copy(src, dst, c_here.at[j])
        return move(src, dst, c_send.at[j], c_recv.at[j], 2 * chip + 1 - core)

    def head_out(kind, j, here):
        buf, land = ((att_buf, att_out), (gq_buf, gq_out))[kind]
        who = core if here else 1 - core
        src = buf.at[aligned(who * rows, rows), columns(j * wide, wide)]
        dst = land.at[:, columns((core * half + j * copies) * D, wide)]
        if here:
            return pltpu.make_async_copy(src, dst, o_here.at[kind, j])
        return move(src, dst, o_send.at[kind, j], o_recv.at[kind, j], 2 * chip + 1 - core)

    def part_out(j, w):
        return move(
            part_kv.at[j, w], got_kv.at[j, w], p_send.at[j, w], p_recv.at[j, w],
            2 * (chip - back + w) + core,
        )

    def pair_out(kind, here):
        who = core if here else 1 - core
        src = fin_kv.at[kind, aligned(who * rows, rows), :]
        dst = kvg_out.at[:, columns((kind * KEY_VALUE_HEADS + core * pairs) * D, pairs * D)]
        if here:
            return pltpu.make_async_copy(src, dst, f_here.at[kind])
        return move(src, dst, f_send.at[kind], f_recv.at[kind], 2 * chip + 1 - core)

    def sums_dp(o):
        return pltpu.make_async_remote_copy(
            src_ref=sums, dst_ref=dp_buf.at[mine],
            send_sem=dp_send.at[o], recv_sem=dp_recv.at[o],
            device_id={"dp": dp_peer(o)}, device_id_type=MESH,
        )

    def sums_sp(o):
        return move(total, gb_all.at[me], gb_send.at[o], gb_recv.at[o], sp_peer(o))

    barrier = pltpu.get_barrier_semaphore()
    for o in range(1, n):
        pl.semaphore_signal(barrier, inc=1, device_id={"sp": sp_peer(o)}, device_id_type=MESH)
    for o in range(1, ndp):
        pl.semaphore_signal(barrier, inc=1, device_id={"dp": dp_peer(o)}, device_id_type=MESH)

    def one_hot(length, source):
        sub = lax.broadcasted_iota(jnp.int32, (PAGE, length), 0)
        lane = lax.broadcasted_iota(jnp.int32, (PAGE, length), 1)
        return jnp.where(lane - sub == source, 1.0, 0.0).astype(jnp.bfloat16)

    for d in range(n):
        slot = jnp.int32(0)
        for i in range(pages_dev):
            page = page_ref[0, d * pages_dev + i]
            slot = slot + jnp.where(
                lax.div(page, pages_dev) == me, lax.rem(page, pages_dev) * PAGE, 0
            )
        perm_out[d * PAGE : (d + 1) * PAGE, :] = one_hot(rows, slot)
    out_kv[:, : back * share, :] = jnp.zeros(
        (2 * KEY_VALUE_HEADS, back * share, D), jnp.bfloat16
    )
    pl.semaphore_wait(barrier, n - 1 + ndp - 1)

    for kind in range(2):
        base = (key_base, value_base)[kind]
        ordered = dot(perm_out[...], proj_ref[:, base : base + KEY_VALUE_HEADS * D])
        for i in range(KEY_VALUE_HEADS):
            out_kv[kind * KEY_VALUE_HEADS + i, back * share :, :] = ordered[
                :, i * D : (i + 1) * D
            ].astype(jnp.bfloat16)

    def send_pair(j, carry):
        for kind in range(2):
            for o in range(n):
                pair_in(kind, j, o).start()
        upstream_in(j, True).start()
        upstream_in(j, False).start()
        for side in range(2):
            first = side * half + j * copies
            ordered = dot(perm_out[...], proj_ref[:, columns(first * D, wide)])
            for i in range(copies):
                out_q[first + i] = ordered[:, i * D : (i + 1) * D].astype(jnp.bfloat16)
        for o in range(n):
            query_in(j, o).start()
        return carry

    lax.fori_loop(0, pairs, send_pair, 0)

    starts = []
    begin = jnp.int32(0)
    for s in range(len_ref.shape[1] - 1):
        begin = begin + len_ref[0, s]
        starts.append(begin)

    def first_of(token):
        first = jnp.zeros_like(token)
        for start in starts:
            first = jnp.where(token >= start, start, first)
        return first

    low = (chip - back) * tokens

    def table_block(i, carry):
        at = aligned(i * 128, 128)
        token = lax.broadcasted_iota(jnp.int32, (128, D), 0) + (i * 128 + low)
        lane = lax.broadcasted_iota(jnp.int32, (128, D), 1)
        angle = (token - first_of(token)).astype(jnp.float32) * freq_ref[...]
        cos_t[at, :] = jnp.cos(angle)
        sine = jnp.sin(angle)
        sin_t[at, :] = jnp.where(lane < D // 2, -sine, sine)
        return carry

    lax.fori_loop(0, span // 128, table_block, 0)

    query_token = lax.broadcasted_iota(jnp.int32, (1, tokens), 1) + chip * tokens
    query_first = first_of(query_token)
    for w in range(back + 1):
        key_token = lax.broadcasted_iota(jnp.int32, (tokens, tokens), 0) + (low + w * tokens)
        keep = (key_token >= query_first) & (key_token <= query_token)
        mask_t[w * tokens : (w + 1) * tokens, :] = jnp.where(keep, 0.0, -jnp.inf)
        for i in range(2 * pages_dev):
            at = jnp.maximum((chip - back + w) * 2 * pages_dev + i, 0)
            source = lax.div(page_ref[0, at], pages_dev)
            inner = i // pages_dev * PAGE
            place = pl.ds(w * tokens + i * PAGE, PAGE)
            perm_kv[place, :] = one_hot(
                n * (back + 1) * share, source * ((back + 1) * share) + w * share + inner
            )
            if w == back:
                perm_q[i * PAGE : (i + 1) * PAGE, :] = one_hot(tokens, source * share + inner)

    def rope(x, at):
        return x * cos_t[at, :] + pltpu.roll(x, D // 2, 1) * sin_t[at, :]

    def unrope(x, at):
        return x * cos_t[at, :] - pltpu.roll(x, D // 2, 1) * sin_t[at, :]

    sums[...] = jnp.zeros_like(sums)

    def one_pair(j, carry):
        for kind in range(2):
            for o in range(n):
                copy = pair_in(kind, j, o)
                copy.wait() if o == 0 else copy.wait_recv()
        key_bias = bias_ref[pl.ds(QUERY_HEADS + core * pairs + j, 1), :]
        value_bias = bias_ref[pl.ds(QUERY_HEADS + KEY_VALUE_HEADS + core * pairs + j, 1), :]
        for w in range(back + 1):
            at = slice(w * tokens, (w + 1) * tokens)
            rotated = rope(dot(perm_kv[at, :], recv_kv[0, j]) + key_bias, at)
            key_rows[at, :] = rotated.astype(jnp.bfloat16)
            key_t[:, at] = rotated.T.astype(jnp.bfloat16)
            shifted = dot(perm_kv[at, :], recv_kv[1, j]) + value_bias
            value_rows[at, :] = shifted.astype(jnp.bfloat16)
            value_t[:, at] = shifted.T.astype(jnp.bfloat16)
        dk[...] = jnp.zeros_like(dk)
        dv[...] = jnp.zeros_like(dv)
        for o in range(n):
            copy = query_in(j, o)
            copy.wait() if o == 0 else copy.wait_recv()
        upstream_in(j, True).wait()
        upstream_in(j, False).wait_recv()

        def two_heads(step, inner):
            for part in range(2):
                h = j * copies + step * 2 + part
                cols = columns(h * D, D)
                query_bias = bias_ref[pl.ds(core * half + h, 1), :]
                query = rope(dot(perm_q[...], recv_q[h]) + query_bias, query_at)
                query = query.astype(jnp.bfloat16)
                upstream = recv_c[:, cols]
                upstream_t = upstream.astype(jnp.float32).T
                scores = dot(key_rows[...], query, NT) * scale
                weights = jnp.exp(scores + mask_t[...])
                totals = jnp.sum(weights, 0, keepdims=True)
                shrink = jnp.where(totals > 1e37, 0.015625, 1.0)
                probs = (weights * shrink) * (1.0 / (totals * shrink))
                rounded = probs.astype(jnp.bfloat16)
                attended_t = dot(value_t[...], rounded)
                att_buf[:, cols] = attended_t.T.astype(jnp.bfloat16)
                kept = attended_t.astype(jnp.bfloat16).astype(jnp.float32)
                delta = jnp.sum(upstream_t * kept, 0, keepdims=True)
                dprobs = dot(value_rows[...], upstream, NT)
                dscores = (probs * (dprobs - delta)).astype(jnp.bfloat16)
                grad_query = unrope(dot(key_t[...], dscores).T * scale, query_at)
                grad_query = grad_query.astype(jnp.bfloat16)
                gq_buf[:, cols] = grad_query
                sums[pl.ds(h, 1), :] = jnp.sum(grad_query.astype(jnp.float32), 0, keepdims=True)
                dk[...] += dot(dscores, query)
                dv[...] += dot(rounded, upstream)
            return inner

        lax.fori_loop(0, copies // 2, two_heads, 0)
        for w in range(back):
            at = slice(w * tokens, (w + 1) * tokens)
            part_kv[j, w, 0] = dk[at, :].astype(jnp.bfloat16)
            part_kv[j, w, 1] = dv[at, :].astype(jnp.bfloat16)

            @pl.when(chip - back + w >= 0)
            def _():
                part_out(j, w).start()

        own_kv[j, 0] = dk[home:, :]
        own_kv[j, 1] = dv[home:, :]
        for kind in range(2):
            head_out(kind, j, True).start()
            head_out(kind, j, False).start()
        return carry

    lax.fori_loop(0, pairs, one_pair, 0)

    for j in range(pairs):
        for w in range(back):

            @pl.when(chip + back - w < chips)
            def _():
                part_out(j, w).wait_recv()
                own_kv[j] = own_kv[j] + got_kv[j, w].astype(jnp.float32)

        grad_key = unrope(own_kv[j, 0] * scale, query_at).astype(jnp.bfloat16)
        grad_value = own_kv[j, 1].astype(jnp.bfloat16)
        fin_kv[0, :, j * D : (j + 1) * D] = grad_key
        fin_kv[1, :, j * D : (j + 1) * D] = grad_value
        sums[half + j : half + j + 1, :] = jnp.sum(grad_key.astype(jnp.float32), 0, keepdims=True)
        sums[half + pairs + j : half + pairs + j + 1, :] = jnp.sum(
            grad_value.astype(jnp.float32), 0, keepdims=True
        )
    for o in range(1, ndp):
        sums_dp(o).start()
    for kind in range(2):
        pair_out(kind, True).start()
        pair_out(kind, False).start()
    dp_buf[mine] = sums[...]
    for o in range(1, ndp):
        sums_dp(o).wait()
    running = dp_buf[0]
    for d in range(1, ndp):
        running = running + dp_buf[d]
    total[...] = running
    for o in range(1, n):
        sums_sp(o).start()
    gb_all[me] = running
    for o in range(1, n):
        sums_sp(o).wait()
    for k in range(2):
        running = gb_all[k]
        for c in range(1, chips):
            running = running + gb_all[2 * c + k]
        gb_out[k * half : (k + 1) * half, :] = running[:half]
        at = QUERY_HEADS + k * pairs
        gb_out[at : at + pairs, :] = running[half : half + pairs]
        at = QUERY_HEADS + KEY_VALUE_HEADS + k * pairs
        gb_out[at : at + pairs, :] = running[half + pairs : half + 2 * pairs]

    for kind in range(2):
        pair_out(kind, True).wait()
        pair_out(kind, False).wait()

    def drain(j, carry):
        for o in range(1, n):
            for kind in range(2):
                pair_in(kind, j, o).wait_send()
            query_in(j, o).wait_send()
        upstream_in(j, False).wait_send()
        for kind in range(2):
            head_out(kind, j, True).wait()
            head_out(kind, j, False).wait()
        for w in range(back):

            @pl.when(chip - back + w >= 0)
            def _():
                part_out(j, w).wait_send()

        return carry

    lax.fori_loop(0, pairs, drain, 0)


def fused_shards(projected, bias, cotangent, lengths, page_source):
    rows, _ = projected.shape
    n = lax.axis_size("sp")
    ndp = lax.axis_size("dp")
    tokens = 2 * rows
    group = n * rows
    back = (group // 2 - 1 + tokens - 1) // tokens
    span = (back + 1) * tokens
    half = QUERY_HEADS // 2
    pairs = KEY_VALUE_HEADS // 2
    share = 2 * PAGE
    exponent = jnp.arange(D // 2, dtype=jnp.float32) * 2.0 / D
    frequency = jnp.power(jnp.float32(rope_base), -exponent)
    frequency = jnp.concatenate([frequency, frequency])[None, :]
    sum_rows = half + 2 * pairs
    f32, bf16 = jnp.float32, jnp.bfloat16
    dma = pltpu.SemaphoreType.DMA
    anywhere = pl.BlockSpec(memory_space=pl.ANY)
    scalars = pl.BlockSpec(memory_space=pltpu.SMEM)
    vector = pl.BlockSpec(memory_space=pltpu.VMEM)
    attended, grad_query, pair_gradient, bias_sums = pl.pallas_call(
        functools.partial(fused_kernel, n, ndp, rows),
        out_shape=(
            jax.ShapeDtypeStruct((rows, QUERY_HEADS * D), bf16),
            jax.ShapeDtypeStruct((rows, QUERY_HEADS * D), bf16),
            jax.ShapeDtypeStruct((rows, 2 * KEY_VALUE_HEADS * D), bf16),
            jax.ShapeDtypeStruct((QUERY_HEADS + 2 * KEY_VALUE_HEADS, D), f32),
        ),
        in_specs=[scalars, scalars, vector, anywhere, vector, vector],
        out_specs=(anywhere, anywhere, anywhere, vector),
        scratch_shapes=[
            pltpu.VMEM((QUERY_HEADS, rows, D), bf16),
            pltpu.VMEM((2 * KEY_VALUE_HEADS, back * share + rows, D), bf16),
            pltpu.VMEM((half, tokens, D), bf16),
            pltpu.VMEM((2, pairs, n * (back + 1) * share, D), bf16),
            pltpu.VMEM((tokens, half * D), bf16),
            pltpu.VMEM((rows, rows), bf16),
            pltpu.VMEM((tokens, tokens), bf16),
            pltpu.VMEM((span, n * (back + 1) * share), bf16),
            pltpu.VMEM((span, D), bf16),
            pltpu.VMEM((span, D), bf16),
            pltpu.VMEM((D, span), bf16),
            pltpu.VMEM((D, span), bf16),
            pltpu.VMEM((span, D), f32),
            pltpu.VMEM((span, D), f32),
            pltpu.VMEM((span, tokens), f32),
            pltpu.VMEM((tokens, half * D), bf16),
            pltpu.VMEM((tokens, half * D), bf16),
            pltpu.VMEM((span, D), f32),
            pltpu.VMEM((span, D), f32),
            pltpu.VMEM((pairs, 2, tokens, D), f32),
            pltpu.VMEM((pairs, back, 2, tokens, D), bf16),
            pltpu.VMEM((pairs, back, 2, tokens, D), bf16),
            pltpu.VMEM((2, tokens, pairs * D), bf16),
            pltpu.VMEM((sum_rows, D), f32),
            pltpu.VMEM((ndp, sum_rows, D), f32),
            pltpu.VMEM((sum_rows, D), f32),
            pltpu.VMEM((n, sum_rows, D), f32),
            dma((2, pairs, n)), dma((2, pairs, n)), dma((pairs, n)), dma((pairs, n)),
            dma((pairs,)), dma((pairs,)), dma((pairs,)),
            dma((2, pairs)), dma((2, pairs)), dma((2, pairs)),
            dma((pairs, back)), dma((pairs, back)),
            dma((2,)), dma((2,)), dma((2,)),
            dma((ndp,)), dma((ndp,)), dma((n,)), dma((n,)),
        ],
        compiler_params=pltpu.CompilerParams(
            collective_id=0, has_side_effects=True, vmem_limit_bytes=56 * 1024 * 1024
        ),
        cost_estimate=pl.CostEstimate(
            flops=14 * half * tokens * span * D,
            bytes_accessed=4 * rows * 36864,
            transcendentals=half * tokens * span,
        ),
    )(lengths, page_source, projected, cotangent, bias.reshape(-1, D), frequency)
    return attended, grad_query, pair_gradient, bias_sums.reshape(-1)


def solution(mesh):
    in_specs = (P(("dp", "sp"), None), P(), P(("dp", "sp"), None), P("dp", None), P("dp", None))
    out_specs = (P(("dp", "sp"), None), P(("dp", "sp"), None), P(("dp", "sp"), None), P())
    body = fused_shards if mesh.shape["sp"] == KEY_VALUE_HEADS else shards
    return jax.shard_map(body, mesh=mesh, in_specs=in_specs, out_specs=out_specs, check_vma=False)
```

```python
import functools

import jax
import jax.numpy as jnp
from jax import lax
from jax.experimental import pallas as pl
from jax.experimental.pallas import tpu as pltpu
from jax.sharding import PartitionSpec as P

QUERY_HEADS = 64
KEY_VALUE_HEADS = 8
HEAD_DIMENSION = 128
PAGE = 16
QBLK = 512


rope_base = 1000000.0


def rope_tables(positions, head_size):
    half_size = head_size // 2
    exponent = jnp.arange(half_size, dtype=jnp.float32) * 2.0 / head_size
    frequency = jnp.power(jnp.float32(rope_base), -exponent)
    angles = positions.astype(jnp.float32)[:, None] * frequency[None, :]
    cosine_table = jnp.cos(angles)
    sine_table = jnp.sin(angles)
    return (
        jnp.concatenate([cosine_table, cosine_table], 1),
        jnp.concatenate([sine_table, sine_table], 1),
    )


def turn_half(tensor_in):
    half_size = tensor_in.shape[-1] // 2
    return jnp.concatenate([-tensor_in[..., half_size:], tensor_in[..., :half_size]], -1)


def apply_rotary(tensor_in, cosine_table, sine_table):
    return tensor_in * cosine_table[:, None, :] + turn_half(tensor_in) * sine_table[:, None, :]


def unrotate(tensor_in, cosine_table, sine_table):
    return tensor_in * cosine_table[:, None, :] - turn_half(tensor_in) * sine_table[:, None, :]


def segments_of(seq_lengths, token_total_count):
    seq_ends = jnp.cumsum(seq_lengths)
    seq_starts = seq_ends - seq_lengths
    tokens_at = jnp.arange(token_total_count, dtype=jnp.int32)
    segment = jnp.sum((tokens_at[:, None] >= seq_ends[None, :]).astype(jnp.int32), 1)
    labels = jnp.arange(seq_lengths.shape[0], dtype=jnp.int32)
    first_token = jnp.sum(jnp.where(segment[:, None] == labels[None, :], seq_starts[None, :], 0), 1)
    return (segment, tokens_at - first_token, first_token)


def shards(projected, bias, cotangent, lengths, page_source):
    shard_rows, row_width = projected.shape
    partition_count = lax.axis_size("sp")
    my_index = lax.axis_index("sp")
    group_rows = shard_rows * partition_count
    pages_dev = shard_rows // PAGE
    query_span_width = QUERY_HEADS * HEAD_DIMENSION
    key_value_width = KEY_VALUE_HEADS * HEAD_DIMENSION
    heads_dev = QUERY_HEADS // partition_count
    head_copies = partition_count // KEY_VALUE_HEADS
    page_table = page_source[0]
    page_grid = page_table.reshape(partition_count, pages_dev)
    source_dev = page_grid // pages_dev
    source_slot = page_grid % pages_dev
    from_here = source_dev == my_index
    pick_slot = jnp.sum(jnp.where(from_here, source_slot, 0), 1)
    present = jnp.any(from_here, 1)
    local_pages = projected.reshape(pages_dev, PAGE, row_width)
    outgoing = jnp.where(
        present[:, None, None], local_pages[pick_slot], jnp.zeros((), projected.dtype)
    )
    incoming = lax.all_to_all(outgoing, "sp", split_axis=0, concat_axis=0, tiled=True)
    own_sources = lax.dynamic_slice_in_dim(source_dev, my_index, 1, 0)[0]
    trainer_rows = incoming[own_sources].reshape(shard_rows, row_width)
    query_part = trainer_rows[:, :query_span_width]
    key_part = trainer_rows[:, query_span_width : query_span_width + key_value_width].reshape(
        shard_rows, KEY_VALUE_HEADS, 1, HEAD_DIMENSION
    )
    value_portion = trainer_rows[:, query_span_width + key_value_width :].reshape(
        shard_rows, KEY_VALUE_HEADS, 1, HEAD_DIMENSION
    )
    joined_rows = jnp.concatenate([key_part, value_portion], 3)
    repeated_heads = jnp.broadcast_to(
        joined_rows, (shard_rows, KEY_VALUE_HEADS, head_copies, 2 * HEAD_DIMENSION)
    ).reshape(shard_rows, partition_count * 2 * HEAD_DIMENSION)
    head_query, head_pair, head_upstream = (
        lax.all_to_all(query_part, "sp", split_axis=1, concat_axis=0, tiled=True),
        lax.all_to_all(repeated_heads, "sp", split_axis=1, concat_axis=0, tiled=True),
        lax.all_to_all(cotangent, "sp", split_axis=1, concat_axis=0, tiled=True),
    )
    kv_head = my_index // head_copies
    query_bias = lax.dynamic_slice_in_dim(
        bias, my_index * heads_dev * HEAD_DIMENSION, heads_dev * HEAD_DIMENSION
    )
    key_bias = lax.dynamic_slice_in_dim(
        bias, query_span_width + kv_head * HEAD_DIMENSION, HEAD_DIMENSION
    )
    value_bias = lax.dynamic_slice_in_dim(
        bias, query_span_width + key_value_width + kv_head * HEAD_DIMENSION, HEAD_DIMENSION
    )
    segment, position, first_token = segments_of(lengths[0], group_rows)
    cosine_table, sine_table = rope_tables(position, HEAD_DIMENSION)
    query_matrix = head_query.astype(jnp.float32).reshape(
        group_rows, heads_dev, HEAD_DIMENSION
    ) + query_bias.reshape(heads_dev, HEAD_DIMENSION)
    query_matrix = apply_rotary(query_matrix, cosine_table, sine_table).astype(jnp.bfloat16)
    key_rows = head_pair[:, :HEAD_DIMENSION].astype(jnp.float32) + key_bias
    key_rows = apply_rotary(key_rows[:, None, :], cosine_table, sine_table)[:, 0].astype(
        jnp.bfloat16
    )
    value_rows = (head_pair[:, HEAD_DIMENSION:].astype(jnp.float32) + value_bias).astype(
        jnp.bfloat16
    )
    block_count = group_rows // QBLK
    score_scale = HEAD_DIMENSION ** (-0.5)
    query_blocks = query_matrix.reshape(block_count, QBLK, heads_dev, HEAD_DIMENSION)
    key_blocks = key_rows.reshape(block_count, QBLK, HEAD_DIMENSION)
    value_blocks = value_rows.reshape(block_count, QBLK, HEAD_DIMENSION)
    segment_blocks = segment.reshape(block_count, QBLK)
    token_blocks = jnp.arange(group_rows, dtype=jnp.int32).reshape(block_count, QBLK)
    upstream_gradient = head_upstream.reshape(block_count, QBLK, heads_dev, HEAD_DIMENSION)

    def weights(row_block, col_block):
        scores = (
            jnp.einsum(
                "qhd,kd->hqk",
                query_blocks[row_block],
                key_blocks[col_block],
                preferred_element_type=jnp.float32,
            )
            * score_scale
        )
        keep = (segment_blocks[row_block][:, None] == segment_blocks[col_block][None, :]) & (
            token_blocks[row_block][:, None] >= token_blocks[col_block][None, :]
        )
        return jnp.where(keep[None], jnp.exp(scores), 0.0)

    zero_rows = jnp.zeros((heads_dev, QBLK), jnp.float32)
    totals = []
    for row_block in range(block_count):
        running = zero_rows
        for col_block in range(row_block + 1):
            running = running + jnp.sum(weights(row_block, col_block), 2)
        totals.append(running)
    zero_out = jnp.zeros((QBLK, heads_dev, HEAD_DIMENSION), jnp.float32)
    attended_blocks = []
    for row_block in range(block_count):
        running = zero_out
        for col_block in range(row_block + 1):
            attend_probs = (weights(row_block, col_block) / totals[row_block][:, :, None]).astype(
                jnp.bfloat16
            )
            running = running + jnp.einsum(
                "hqk,kd->qhd",
                attend_probs,
                value_blocks[col_block],
                preferred_element_type=jnp.float32,
            )
        attended_blocks.append(running.astype(jnp.bfloat16))
    attended = jnp.stack(attended_blocks)
    attended_out = lax.all_to_all(
        attended.reshape(group_rows, heads_dev * HEAD_DIMENSION),
        "sp",
        split_axis=0,
        concat_axis=1,
        tiled=True,
    )
    zero_key = jnp.zeros((QBLK, HEAD_DIMENSION), jnp.float32)
    key_grads = [zero_key for col_block in range(block_count)]
    value_grads = [zero_key for col_block in range(block_count)]
    query_grads = []
    for row_block in range(block_count):
        delta = jnp.transpose(
            jnp.sum(
                upstream_gradient[row_block].astype(jnp.float32)
                * attended[row_block].astype(jnp.float32),
                2,
            )
        )
        running = zero_out
        for col_block in range(row_block + 1):
            probs = weights(row_block, col_block) / totals[row_block][:, :, None]
            rounded = probs.astype(jnp.bfloat16)
            dprobs = jnp.einsum(
                "qhd,kd->hqk",
                upstream_gradient[row_block],
                value_blocks[col_block],
                preferred_element_type=jnp.float32,
            )
            dscores = (probs * (dprobs - delta[:, :, None])).astype(jnp.bfloat16)
            part_query = (
                jnp.einsum(
                    "hqk,kd->qhd",
                    dscores,
                    key_blocks[col_block],
                    preferred_element_type=jnp.float32,
                )
                * score_scale
            )
            part_key = (
                jnp.einsum(
                    "hqk,qhd->kd",
                    dscores,
                    query_blocks[row_block],
                    preferred_element_type=jnp.float32,
                )
                * score_scale
            )
            part_value = jnp.einsum(
                "hqk,qhd->kd",
                rounded,
                upstream_gradient[row_block],
                preferred_element_type=jnp.float32,
            )
            part_query, part_key, part_value = (part_query, part_key, part_value)
            running = running + part_query
            key_grads[col_block] = key_grads[col_block] + part_key
            value_grads[col_block] = value_grads[col_block] + part_value
        query_grads.append(running)
    rot_query = jnp.stack(query_grads).reshape(group_rows, heads_dev, HEAD_DIMENSION)
    grad_query = (
        unrotate(rot_query, cosine_table, sine_table)
        .astype(jnp.bfloat16)
        .reshape(group_rows, heads_dev * HEAD_DIMENSION)
    )
    query_out = lax.all_to_all(grad_query, "sp", split_axis=0, concat_axis=1, tiled=True)
    grad_key = unrotate(
        jnp.stack(key_grads).reshape(group_rows, 1, HEAD_DIMENSION), cosine_table, sine_table
    ).reshape(group_rows, HEAD_DIMENSION)
    grad_value = jnp.stack(value_grads).reshape(group_rows, HEAD_DIMENSION)
    pair_grads = jnp.concatenate([grad_key, grad_value], 1)
    pair_gradient_back = lax.all_to_all(pair_grads, "sp", split_axis=0, concat_axis=1, tiled=True)
    pair_gradient_sum = jnp.sum(
        pair_gradient_back.reshape(shard_rows, KEY_VALUE_HEADS, head_copies, 2, HEAD_DIMENSION), 2
    )
    key_value_gradient = (
        jnp.transpose(pair_gradient_sum, (0, 2, 1, 3))
        .reshape(shard_rows, 2 * key_value_width)
        .astype(jnp.bfloat16)
    )
    local_sums = jnp.concatenate(
        [
            jnp.sum(query_out.astype(jnp.float32), 0),
            jnp.sum(key_value_gradient.astype(jnp.float32), 0),
        ]
    )
    grad_bias = lax.psum(local_sums, ("dp", "sp"))
    return (attended_out, query_out, key_value_gradient, grad_bias)


MESH = pl.DeviceIdType.MESH
D = HEAD_DIMENSION
LOG2E = 1.4426950408889634
NT = (((1,), (1,)), ((), ()))
NN = (((1,), (0,)), ((), ()))


def dot(left, right, dims=NN):
    return lax.dot_general(left, right, dims, preferred_element_type=jnp.float32)


def fused_kernel(
    n, ndp, rows,
    len_ref, page_ref, proj_ref, cot_ref, bias_ref, freq_ref,
    att_out, gq_out, kvg_out, gb_out,
    out_q, out_kv, recv_q, recv_kv, recv_c, perm_out, perm_q, perm_kv,
    key_rows, value_rows, key_t, value_t, cos_t, sin_t, mask_t, att_buf, gq_buf,
    dk, dv, own_kv, part_kv, got_kv, fin_kv, sums, dp_buf, total, gb_all,
    kv_send, kv_recv, q_send, q_recv, c_send, c_recv, c_here,
    o_send, o_recv, o_here, p_send, p_recv, f_send, f_recv, f_here,
    dp_send, dp_recv, gb_send, gb_recv,
):
    me = lax.axis_index("sp")
    mine = lax.axis_index("dp")
    chip, core = me // 2, lax.rem(me, 2)
    chips = n // 2
    tokens = 2 * rows
    group = n * rows
    share = 2 * PAGE
    pages_dev = rows // PAGE
    back = (group // 2 - 1 + tokens - 1) // tokens
    span = (back + 1) * tokens
    home = back * tokens
    half = QUERY_HEADS // 2
    pairs = KEY_VALUE_HEADS // 2
    copies = half // pairs
    wide = copies * D
    steps = copies // 2
    part_rows = tokens // 2
    window = group // 2
    scale = D ** (-0.5)
    key_base = QUERY_HEADS * D
    value_base = key_base + KEY_VALUE_HEADS * D
    query_at = slice(home, span)
    reach = [
        (max(0, (home + u * part_rows - window + 1) // part_rows * part_rows), home + (u + 1) * part_rows)
        for u in range(2)
    ]

    def aligned(start, size):
        return pl.ds(pl.multiple_of(start, size), size)

    def columns(start, size):
        return pl.ds(pl.multiple_of(start, D), size)

    def sp_peer(o):
        return lax.rem(me + o, n)

    def dp_peer(o):
        return lax.rem(mine + o, ndp)

    def move(src, dst, send, recv, target):
        return pltpu.make_async_remote_copy(
            src_ref=src, dst_ref=dst, send_sem=send, recv_sem=recv,
            device_id={"sp": target}, device_id_type=MESH,
        )

    def pair_in(kind, j, o):
        peer = sp_peer(o)
        src = out_kv.at[
            kind * KEY_VALUE_HEADS + lax.rem(peer, 2) * pairs + j,
            pl.ds(pl.multiple_of(peer // 2 * share, share), (back + 1) * share), :,
        ]
        dst = recv_kv.at[kind, j, aligned(me * (back + 1) * share, (back + 1) * share), :]
        if o == 0:
            return pltpu.make_async_copy(src, dst, kv_recv.at[kind, j, 0])
        return move(src, dst, kv_send.at[kind, j, o], kv_recv.at[kind, j, o], peer)

    def query_in(g, o):
        peer = sp_peer(o)
        src = out_q.at[
            pl.ds(lax.rem(peer, 2) * half + g * 2, 2), aligned(peer // 2 * share, share), :
        ]
        dst = recv_q.at[pl.ds(g * 2, 2), aligned(me * share, share), :]
        if o == 0:
            return pltpu.make_async_copy(src, dst, q_recv.at[g, 0])
        return move(src, dst, q_send.at[g, o], q_recv.at[g, o], peer)

    def upstream_in(j, here):
        who = core if here else 1 - core
        src = cot_ref.at[:, columns((who * half + j * copies) * D, wide)]
        dst = recv_c.at[aligned(core * rows, rows), columns(j * wide, wide)]
        if here:
            return pltpu.make_async_copy(src, dst, c_here.at[j])
        return move(src, dst, c_send.at[j], c_recv.at[j], 2 * chip + 1 - core)

    def head_out(kind, j, here):
        buf, land = ((att_buf, att_out), (gq_buf, gq_out))[kind]
        who = core if here else 1 - core
        src = buf.at[aligned(who * rows, rows), columns(j * wide, wide)]
        dst = land.at[:, columns((core * half + j * copies) * D, wide)]
        if here:
            return pltpu.make_async_copy(src, dst, o_here.at[kind, j])
        return move(src, dst, o_send.at[kind, j], o_recv.at[kind, j], 2 * chip + 1 - core)

    def part_out(j, w):
        return move(
            part_kv.at[j, w], got_kv.at[j, w], p_send.at[j, w], p_recv.at[j, w],
            2 * (chip - back + w) + core,
        )

    def pair_out(kind, here):
        who = core if here else 1 - core
        src = fin_kv.at[kind, aligned(who * rows, rows), :]
        dst = kvg_out.at[:, columns((kind * KEY_VALUE_HEADS + core * pairs) * D, pairs * D)]
        if here:
            return pltpu.make_async_copy(src, dst, f_here.at[kind])
        return move(src, dst, f_send.at[kind], f_recv.at[kind], 2 * chip + 1 - core)

    def sums_dp(o):
        return pltpu.make_async_remote_copy(
            src_ref=sums, dst_ref=dp_buf.at[mine],
            send_sem=dp_send.at[o], recv_sem=dp_recv.at[o],
            device_id={"dp": dp_peer(o)}, device_id_type=MESH,
        )

    def sums_sp(o):
        return move(total, gb_all.at[me], gb_send.at[o], gb_recv.at[o], sp_peer(o))

    barrier = pltpu.get_barrier_semaphore()
    for o in range(1, n):
        pl.semaphore_signal(barrier, inc=1, device_id={"sp": sp_peer(o)}, device_id_type=MESH)
    for o in range(1, ndp):
        pl.semaphore_signal(barrier, inc=1, device_id={"dp": dp_peer(o)}, device_id_type=MESH)

    def one_hot(length, source):
        sub = lax.broadcasted_iota(jnp.int32, (PAGE, length), 0)
        lane = lax.broadcasted_iota(jnp.int32, (PAGE, length), 1)
        return jnp.where(lane - sub == source, 1.0, 0.0).astype(jnp.bfloat16)

    for d in range(n):
        slot = jnp.int32(0)
        for i in range(pages_dev):
            page = page_ref[0, d * pages_dev + i]
            slot = slot + jnp.where(
                lax.div(page, pages_dev) == me, lax.rem(page, pages_dev) * PAGE, 0
            )
        perm_out[d * PAGE : (d + 1) * PAGE, :] = one_hot(rows, slot)
    out_kv[:, : back * share, :] = jnp.zeros(
        (2 * KEY_VALUE_HEADS, back * share, D), jnp.bfloat16
    )
    pl.semaphore_wait(barrier, n - 1 + ndp - 1)

    for kind in range(2):
        base = (key_base, value_base)[kind]
        ordered = dot(perm_out[...], proj_ref[:, base : base + KEY_VALUE_HEADS * D])
        for i in range(KEY_VALUE_HEADS):
            out_kv[kind * KEY_VALUE_HEADS + i, back * share :, :] = ordered[
                :, i * D : (i + 1) * D
            ].astype(jnp.bfloat16)

    def send_pair(j, carry):
        for kind in range(2):
            for o in range(n):
                pair_in(kind, j, o).start()
        upstream_in(j, True).start()
        upstream_in(j, False).start()
        for side in range(2):
            first = side * half + j * copies
            ordered = dot(perm_out[...], proj_ref[:, columns(first * D, wide)])
            for i in range(copies):
                out_q[first + i] = ordered[:, i * D : (i + 1) * D].astype(jnp.bfloat16)
        for step in range(steps):
            for o in range(n):
                query_in(j * steps + step, o).start()
        return carry

    lax.fori_loop(0, pairs, send_pair, 0)

    starts = []
    begin = jnp.int32(0)
    for s in range(len_ref.shape[1] - 1):
        begin = begin + len_ref[0, s]
        starts.append(begin)

    def first_of(token):
        first = jnp.zeros_like(token)
        for start in starts:
            first = jnp.where(token >= start, start, first)
        return first

    low = (chip - back) * tokens

    def table_block(i, carry):
        at = aligned(i * 128, 128)
        token = lax.broadcasted_iota(jnp.int32, (128, D), 0) + (i * 128 + low)
        lane = lax.broadcasted_iota(jnp.int32, (128, D), 1)
        angle = (token - first_of(token)).astype(jnp.float32) * freq_ref[...]
        cos_t[at, :] = jnp.cos(angle)
        sine = jnp.sin(angle)
        sin_t[at, :] = jnp.where(lane < D // 2, -sine, sine)
        return carry

    lax.fori_loop(0, span // 128, table_block, 0)

    for u in range(2):
        first_key, last_key = reach[u]
        lane = lax.broadcasted_iota(jnp.int32, (1, tokens), 1)
        lane = jnp.where(lane >= part_rows, lane - part_rows, lane)
        query_token = lane + (chip * tokens + u * part_rows)
        query_first = first_of(query_token)
        for part in range(first_key, last_key, part_rows):
            key_token = lax.broadcasted_iota(jnp.int32, (part_rows, tokens), 0) + (low + part)
            keep = (key_token >= query_first) & (key_token <= query_token)
            mask_t[u, part - first_key : part - first_key + part_rows, :] = jnp.where(
                keep, 0.0, -jnp.inf
            )
    for w in range(back + 1):
        for i in range(2 * pages_dev):
            at = jnp.maximum((chip - back + w) * 2 * pages_dev + i, 0)
            source = lax.div(page_ref[0, at], pages_dev)
            inner = i // pages_dev * PAGE
            place = pl.ds(w * tokens + i * PAGE, PAGE)
            perm_kv[place, :] = one_hot(
                n * (back + 1) * share, source * ((back + 1) * share) + w * share + inner
            )
            if w == back:
                perm_q[i * PAGE : (i + 1) * PAGE, :] = one_hot(tokens, source * share + inner)

    def rope(x, at):
        return x * cos_t[at, :] + pltpu.roll(x, D // 2, 1) * sin_t[at, :]

    def unrope(x, at):
        return x * cos_t[at, :] - pltpu.roll(x, D // 2, 1) * sin_t[at, :]

    sums[...] = jnp.zeros_like(sums)

    def one_pair(j, carry):
        for kind in range(2):
            for o in range(n):
                copy = pair_in(kind, j, o)
                copy.wait() if o == 0 else copy.wait_recv()
        key_bias = bias_ref[pl.ds(QUERY_HEADS + core * pairs + j, 1), :]
        value_bias = bias_ref[pl.ds(QUERY_HEADS + KEY_VALUE_HEADS + core * pairs + j, 1), :]
        for w in range(back + 1):
            at = slice(w * tokens, (w + 1) * tokens)
            pair = dot(perm_kv[at, :], jnp.concatenate([recv_kv[0, j], recv_kv[1, j]], 1))
            rotated = rope(pair[:, :D] + key_bias, at)
            key_rows[at, :] = rotated.astype(jnp.bfloat16)
            key_t[:, at] = rotated.T.astype(jnp.bfloat16)
            shifted = pair[:, D:] + value_bias
            value_rows[at, :] = shifted.astype(jnp.bfloat16)
            value_t[:, at] = shifted.T.astype(jnp.bfloat16)
        dk[...] = jnp.zeros_like(dk)
        dv[...] = jnp.zeros_like(dv)
        upstream_in(j, True).wait()
        upstream_in(j, False).wait_recv()

        def two_heads(step, inner):
            g = j * steps + step
            for o in range(n):
                copy = query_in(g, o)
                copy.wait() if o == 0 else copy.wait_recv()
            cols = [columns((g * 2 + part) * D, D) for part in range(2)]
            both = dot(perm_q[...], jnp.concatenate([recv_q[g * 2], recv_q[g * 2 + 1]], 1))
            queries = []
            for part in range(2):
                query_bias = bias_ref[pl.ds(core * half + g * 2 + part, 1), :]
                rotated = rope(both[:, part * D : (part + 1) * D] + query_bias, query_at)
                queries.append(rotated.astype(jnp.bfloat16))
            column_sums = [jnp.zeros((1, D), jnp.float32) for part in range(2)]
            for u in range(2):
                at = slice(u * part_rows, (u + 1) * part_rows)
                table_at = slice(home + u * part_rows, home + (u + 1) * part_rows)
                keys = slice(*reach[u])
                query = jnp.concatenate([queries[0][at], queries[1][at]], 0)
                upstream = jnp.concatenate([recv_c[at, cols[0]], recv_c[at, cols[1]]], 0)
                upstream_t = upstream.astype(jnp.float32).T
                scores = dot(key_rows[keys, :], query, NT) * (scale * LOG2E)
                weights = jnp.exp2(scores + mask_t[u])
                totals = jnp.sum(weights, 0, keepdims=True)
                shrink = jnp.where(totals > 1e37, 0.015625, 1.0)
                probs = (weights * shrink) * (1.0 / (totals * shrink))
                rounded = probs.astype(jnp.bfloat16)
                attended_t = dot(value_t[:, keys], rounded)
                attended = attended_t.T.astype(jnp.bfloat16)
                kept = attended_t.astype(jnp.bfloat16).astype(jnp.float32)
                delta = jnp.sum(upstream_t * kept, 0, keepdims=True)
                dprobs = dot(value_rows[keys, :], upstream, NT)
                dscores = (probs * (dprobs - delta)).astype(jnp.bfloat16)
                rot_query = dot(key_t[:, keys], dscores).T * scale
                for part in range(2):
                    rows_at = slice(part * part_rows, (part + 1) * part_rows)
                    att_buf[at, cols[part]] = attended[rows_at]
                    grad_query = unrope(rot_query[rows_at], table_at).astype(jnp.bfloat16)
                    gq_buf[at, cols[part]] = grad_query
                    column_sums[part] += jnp.sum(grad_query.astype(jnp.float32), 0, keepdims=True)
                dk[keys, :] += dot(dscores, query)
                dv[keys, :] += dot(rounded, upstream)
            for part in range(2):
                sums[pl.ds(g * 2 + part, 1), :] = column_sums[part]
            return inner

        lax.fori_loop(0, steps, two_heads, 0)
        for w in range(back):
            at = slice(w * tokens, (w + 1) * tokens)
            part_kv[j, w, 0] = dk[at, :].astype(jnp.bfloat16)
            part_kv[j, w, 1] = dv[at, :].astype(jnp.bfloat16)

            @pl.when(chip - back + w >= 0)
            def _():
                part_out(j, w).start()

        own_kv[j, 0] = dk[home:, :]
        own_kv[j, 1] = dv[home:, :]
        for kind in range(2):
            head_out(kind, j, True).start()
            head_out(kind, j, False).start()
        return carry

    lax.fori_loop(0, pairs, one_pair, 0)

    for j in range(pairs):
        for w in range(back):

            @pl.when(chip + back - w < chips)
            def _():
                part_out(j, w).wait_recv()
                own_kv[j] = own_kv[j] + got_kv[j, w].astype(jnp.float32)

        grad_key = unrope(own_kv[j, 0] * scale, query_at).astype(jnp.bfloat16)
        grad_value = own_kv[j, 1].astype(jnp.bfloat16)
        fin_kv[0, :, j * D : (j + 1) * D] = grad_key
        fin_kv[1, :, j * D : (j + 1) * D] = grad_value
        sums[half + j : half + j + 1, :] = jnp.sum(grad_key.astype(jnp.float32), 0, keepdims=True)
        sums[half + pairs + j : half + pairs + j + 1, :] = jnp.sum(
            grad_value.astype(jnp.float32), 0, keepdims=True
        )
    for o in range(1, ndp):
        sums_dp(o).start()
    for kind in range(2):
        pair_out(kind, True).start()
        pair_out(kind, False).start()
    dp_buf[mine] = sums[...]
    for o in range(1, ndp):
        sums_dp(o).wait()
    running = dp_buf[0]
    for d in range(1, ndp):
        running = running + dp_buf[d]
    total[...] = running
    for o in range(1, n):
        sums_sp(o).start()
    gb_all[me] = running
    for o in range(1, n):
        sums_sp(o).wait()
    for k in range(2):
        running = gb_all[k]
        for c in range(1, chips):
            running = running + gb_all[2 * c + k]
        gb_out[k * half : (k + 1) * half, :] = running[:half]
        at = QUERY_HEADS + k * pairs
        gb_out[at : at + pairs, :] = running[half : half + pairs]
        at = QUERY_HEADS + KEY_VALUE_HEADS + k * pairs
        gb_out[at : at + pairs, :] = running[half + pairs : half + 2 * pairs]

    for kind in range(2):
        pair_out(kind, True).wait()
        pair_out(kind, False).wait()

    def drain(j, carry):
        for o in range(1, n):
            for kind in range(2):
                pair_in(kind, j, o).wait_send()
            for step in range(steps):
                query_in(j * steps + step, o).wait_send()
        upstream_in(j, False).wait_send()
        for kind in range(2):
            head_out(kind, j, True).wait()
            head_out(kind, j, False).wait()
        for w in range(back):

            @pl.when(chip - back + w >= 0)
            def _():
                part_out(j, w).wait_send()

        return carry

    lax.fori_loop(0, pairs, drain, 0)


def fused_shards(projected, bias, cotangent, lengths, page_source):
    rows, _ = projected.shape
    n = lax.axis_size("sp")
    ndp = lax.axis_size("dp")
    tokens = 2 * rows
    group = n * rows
    back = (group // 2 - 1 + tokens - 1) // tokens
    span = (back + 1) * tokens
    half = QUERY_HEADS // 2
    pairs = KEY_VALUE_HEADS // 2
    share = 2 * PAGE
    reach = (group // 2 - 1 + rows - 1) // rows * rows + rows
    exponent = jnp.arange(D // 2, dtype=jnp.float32) * 2.0 / D
    frequency = jnp.power(jnp.float32(rope_base), -exponent)
    frequency = jnp.concatenate([frequency, frequency])[None, :]
    sum_rows = half + 2 * pairs
    f32, bf16 = jnp.float32, jnp.bfloat16
    dma = pltpu.SemaphoreType.DMA
    anywhere = pl.BlockSpec(memory_space=pl.ANY)
    scalars = pl.BlockSpec(memory_space=pltpu.SMEM)
    vector = pl.BlockSpec(memory_space=pltpu.VMEM)
    attended, grad_query, pair_gradient, bias_sums = pl.pallas_call(
        functools.partial(fused_kernel, n, ndp, rows),
        out_shape=(
            jax.ShapeDtypeStruct((rows, QUERY_HEADS * D), bf16),
            jax.ShapeDtypeStruct((rows, QUERY_HEADS * D), bf16),
            jax.ShapeDtypeStruct((rows, 2 * KEY_VALUE_HEADS * D), bf16),
            jax.ShapeDtypeStruct((QUERY_HEADS + 2 * KEY_VALUE_HEADS, D), f32),
        ),
        in_specs=[scalars, scalars, vector, anywhere, vector, vector],
        out_specs=(anywhere, anywhere, anywhere, vector),
        scratch_shapes=[
            pltpu.VMEM((QUERY_HEADS, rows, D), bf16),
            pltpu.VMEM((2 * KEY_VALUE_HEADS, back * share + rows, D), bf16),
            pltpu.VMEM((half, tokens, D), bf16),
            pltpu.VMEM((2, pairs, n * (back + 1) * share, D), bf16),
            pltpu.VMEM((tokens, half * D), bf16),
            pltpu.VMEM((rows, rows), bf16),
            pltpu.VMEM((tokens, tokens), bf16),
            pltpu.VMEM((span, n * (back + 1) * share), bf16),
            pltpu.VMEM((span, D), bf16),
            pltpu.VMEM((span, D), bf16),
            pltpu.VMEM((D, span), bf16),
            pltpu.VMEM((D, span), bf16),
            pltpu.VMEM((span, D), f32),
            pltpu.VMEM((span, D), f32),
            pltpu.VMEM((2, reach, tokens), f32),
            pltpu.VMEM((tokens, half * D), bf16),
            pltpu.VMEM((tokens, half * D), bf16),
            pltpu.VMEM((span, D), f32),
            pltpu.VMEM((span, D), f32),
            pltpu.VMEM((pairs, 2, tokens, D), f32),
            pltpu.VMEM((pairs, back, 2, tokens, D), bf16),
            pltpu.VMEM((pairs, back, 2, tokens, D), bf16),
            pltpu.VMEM((2, tokens, pairs * D), bf16),
            pltpu.VMEM((sum_rows, D), f32),
            pltpu.VMEM((ndp, sum_rows, D), f32),
            pltpu.VMEM((sum_rows, D), f32),
            pltpu.VMEM((n, sum_rows, D), f32),
            dma((2, pairs, n)), dma((2, pairs, n)), dma((half // 2, n)), dma((half // 2, n)),
            dma((pairs,)), dma((pairs,)), dma((pairs,)),
            dma((2, pairs)), dma((2, pairs)), dma((2, pairs)),
            dma((pairs, back)), dma((pairs, back)),
            dma((2,)), dma((2,)), dma((2,)),
            dma((ndp,)), dma((ndp,)), dma((n,)), dma((n,)),
        ],
        compiler_params=pltpu.CompilerParams(
            collective_id=0, has_side_effects=True, vmem_limit_bytes=56 * 1024 * 1024
        ),
        cost_estimate=pl.CostEstimate(
            flops=14 * half * tokens * span * D,
            bytes_accessed=4 * rows * 36864,
            transcendentals=half * tokens * span,
        ),
    )(lengths, page_source, projected, cotangent, bias.reshape(-1, D), frequency)
    return attended, grad_query, pair_gradient, bias_sums.reshape(-1)


def solution(mesh):
    in_specs = (P(("dp", "sp"), None), P(), P(("dp", "sp"), None), P("dp", None), P("dp", None))
    out_specs = (P(("dp", "sp"), None), P(("dp", "sp"), None), P(("dp", "sp"), None), P())
    body = fused_shards if mesh.shape["sp"] == KEY_VALUE_HEADS else shards
    return jax.shard_map(body, mesh=mesh, in_specs=in_specs, out_specs=out_specs, check_vma=False)
```
